128 devices in a mesh: ctx: 32 (over z, y, core), head: 4 (over x).
Axes of the slice: x: 4, y: 4, z: 4, core: 2. Of those that a mesh axis runs over, the one named last changes fastest.
Arguments:
- frames: bfloat16 [65536, 1024], P('ctx'), may hold values from -60 to 60, as said below
- len_keys: bfloat16 [256, 65536], P(None, 'ctx'), may hold values from -0.0234375 to 0.0234375
- len_values: bfloat16 [256, 65536], P(None, 'ctx'), may hold values from -0.0234375 to 0.0234375
- w_query: bfloat16 [1024, 1024], P(None, 'head'), may hold values from -0.1875 to 0.1875
- w_key: bfloat16 [1024, 1024], P(None, 'head'), may hold values from -0.1875 to 0.1875
- w_value: bfloat16 [1024, 1024], P(None, 'head'), may hold values from -0.1875 to 0.1875
- w_out: bfloat16 [1024, 1024], P('head'), may hold values from -0.1875 to 0.1875
- cotangent: bfloat16 [65536, 1024], P('ctx', 'head'), may hold values from -6 to 6
Outputs:
- mixed: bfloat16 [65536, 1024], P('ctx', 'head')
- grad_frames: bfloat16 [65536, 1024], P('ctx', 'head')
- grad_wq: float32 [1024, 1024], P(None, 'head')
- grad_wk: float32 [1024, 1024], P(None, 'head')
- grad_wv: float32 [1024, 1024], P(None, 'head')
- grad_wo: float32 [1024, 1024], P('head')
The draws below stay inside these ranges and needn't reach their ends.
Inputs may be any that keep to these rules, and one draw needn't show every extreme that they name: `frames`: frame features.
All inputs are finite; a program needn't handle non-finite values.
Results may differ from the reference program's by a relative error of at most 0.017.
Values may be sent and summed in bfloat16 or wider, within the bound.
A program may use at most 128 MiB of HBM per device.

```python
import jax
import jax.numpy as jnp

D = 1024
H = 16
DH = 64
KP = 256
FRAMES = 65536


def draw_frames(key, part):
    key = jax.random.fold_in(key, 11)
    return jnp.clip(jax.random.normal(key, (FRAMES, D), jnp.float32), -6.0, 6.0).astype(jnp.bfloat16)


def levels(key, extent, shards, least, high):
    gain, own = 1.0, jax.random.fold_in(key, 6)
    for axis_at, blocks in shards:
        steps = jnp.exp(jax.random.uniform(jax.random.fold_in(own, axis_at), (blocks,), jnp.float32, least / len(shards), high / len(shards)))
        gain = gain * jnp.repeat(steps, extent[axis_at] // blocks).reshape([-1 if axis == axis_at else 1 for axis in range(len(extent))])
    return gain


def noise(stream_key, dims, deviation, most, pieces=(), kind=jnp.bfloat16):
    values = deviation * jax.random.normal(stream_key, dims, jnp.float32)
    if pieces:
        values = values * levels(stream_key, dims, pieces, -0.22, 0.18)
    return jnp.clip(values, -most, most).astype(kind)


def setup_inputs(seed: int = 0) -> dict:
    arg_keys = jax.random.split(jax.random.key(seed), 9)
    return {
        "frames": draw_frames(jax.random.fold_in(arg_keys[8], 71), 0),
        "len_keys": noise(arg_keys[1], (KP, FRAMES), FRAMES ** -0.5, 0.0234375, ((1, 32),)),
        "len_values": noise(arg_keys[2], (KP, FRAMES), FRAMES ** -0.5, 0.0234375, ((1, 32),)),
        "w_query": noise(arg_keys[3], (D, H * DH), D ** -0.5, 0.1875, ((1, 4),)),
        "w_key": noise(arg_keys[4], (D, H * DH), D ** -0.5, 0.1875, ((1, 4),)),
        "w_value": noise(arg_keys[5], (D, H * DH), D ** -0.5, 0.1875, ((1, 4),)),
        "w_out": noise(arg_keys[6], (H * DH, D), (H * DH) ** -0.5, 0.1875, ((0, 4),)),
        "cotangent": noise(arg_keys[7], (FRAMES, D), 1.0, 6.0, ((0, 32), (1, 4))),
    }


def reference(frames, len_keys, len_values, w_query, w_key, w_value, w_out, cotangent):
    scaling = DH ** -0.5
    query = jnp.dot(frames, w_query, preferred_element_type=jnp.float32).astype(jnp.bfloat16)
    keys_full = jnp.dot(frames, w_key, preferred_element_type=jnp.float32).astype(jnp.bfloat16)
    values_full = jnp.dot(frames, w_value, preferred_element_type=jnp.float32).astype(jnp.bfloat16)
    keys_proj = jnp.dot(len_keys, keys_full, preferred_element_type=jnp.float32).astype(jnp.bfloat16)
    values_proj = jnp.dot(len_values, values_full, preferred_element_type=jnp.float32).astype(jnp.bfloat16)
    grad_attn = jnp.dot(cotangent, w_out.T, preferred_element_type=jnp.float32).astype(jnp.bfloat16)
    outs_list = []
    dq_list = []
    dkp_list = []
    dvp_list = []
    for head_idx in range(H):
        lower = head_idx * DH
        upper = lower + DH
        query_h = query[:, lower:upper]
        keys_h = keys_proj[:, lower:upper]
        values_h = values_proj[:, lower:upper]
        scores = jnp.dot(query_h, keys_h.T, preferred_element_type=jnp.float32) * scaling
        probab = jax.nn.softmax(scores, axis=-1)
        probab_b = probab.astype(jnp.bfloat16)
        outs_list.append(jnp.dot(probab_b, values_h, preferred_element_type=jnp.float32).astype(jnp.bfloat16))
        grad_h = grad_attn[:, lower:upper]
        grad_prob = jnp.dot(grad_h, values_h.T, preferred_element_type=jnp.float32)
        dvp_list.append(jnp.dot(probab_b.T, grad_h, preferred_element_type=jnp.float32))
        inner = jnp.sum(probab * grad_prob, axis=-1, keepdims=True)
        grad_score = (probab * (grad_prob - inner) * scaling).astype(jnp.bfloat16)
        dq_list.append(jnp.dot(grad_score, keys_h, preferred_element_type=jnp.float32).astype(jnp.bfloat16))
        dkp_list.append(jnp.dot(grad_score.T, query_h, preferred_element_type=jnp.float32))
    attended = jnp.concatenate(outs_list, axis=1)
    mixed = jnp.dot(attended, w_out, preferred_element_type=jnp.float32).astype(jnp.bfloat16)
    grad_query = jnp.concatenate(dq_list, axis=1)
    grad_kproj = jnp.concatenate(dkp_list, axis=1).astype(jnp.bfloat16)
    grad_vproj = jnp.concatenate(dvp_list, axis=1).astype(jnp.bfloat16)
    grad_keys = jnp.dot(len_keys.T, grad_kproj, preferred_element_type=jnp.float32).astype(jnp.bfloat16)
    grad_values = jnp.dot(len_values.T, grad_vproj, preferred_element_type=jnp.float32).astype(jnp.bfloat16)
    total = jnp.dot(grad_query, w_query.T, preferred_element_type=jnp.float32)
    total = total + jnp.dot(grad_keys, w_key.T, preferred_element_type=jnp.float32)
    total = total + jnp.dot(grad_values, w_value.T, preferred_element_type=jnp.float32)
    grad_frames = total.astype(jnp.bfloat16)
    grad_wq = jnp.dot(frames.T, grad_query, preferred_element_type=jnp.float32)
    grad_wk = jnp.dot(frames.T, grad_keys, preferred_element_type=jnp.float32)
    grad_wv = jnp.dot(frames.T, grad_values, preferred_element_type=jnp.float32)
    grad_wo = jnp.dot(attended.T, cotangent, preferred_element_type=jnp.float32)
    return (mixed, grad_frames, grad_wq, grad_wk, grad_wv, grad_wo)
```

```python
import functools

import jax
import jax.numpy as jnp
from jax import lax
from jax.experimental import pallas as pl
from jax.experimental.pallas import tpu as pltpu
from jax.sharding import PartitionSpec as P

DH = 64
MESH = pl.DeviceIdType.MESH
BF = jnp.bfloat16
F32 = jnp.float32


def dot(a, b):
    return jnp.dot(a, b, preferred_element_type=F32)


def dot_nt(a, b):
    return lax.dot_general(a, b, (((1,), (1,)), ((), ())), preferred_element_type=F32)


def flip(a):
    return a.astype(F32).T.astype(BF)


class Sems:
    def __init__(self, ref):
        self.ref, self.used = ref, 0

    def new(self):
        self.used += 1
        return self.ref.at[self.used - 1]


def kernel(
    frames, len_keys, len_values, w_query, w_key, w_value, w_out, cotangent,
    mixed_o, gframes_o, gwq_o, gwk_o, gwv_o, gwo_o,
    fcols, frows, lens, len_t, wqf, wof, wkv, cot,
    fpart, fpair, fsum, frs, fx, kpx, ff, kvp,
    q, ga, prob, att_t, att, gq_t, gq,
    mix_s, mix_r, gf_s, gf_r,
    gkv, gkv_pair, gkv_sum, gkv_rs, gkv_x, gkv_xr, gk16, m_s, m_r, gkm,
    w_s, w_pair, w_sum, w_rs, w_x, w_xr, w_ag, w_f, sem_ref,
):
    sems = Sems(sem_ref)
    me = lax.axis_index("ctx")
    x = lax.axis_index("head")
    core = lax.rem(me, 2)
    chip = lax.div(me, 2)
    other = me + 1 - 2 * core
    rows = frows.shape[0]
    n_x = 4
    n_chip = 16
    width = 256

    def load(src, dst):
        copy = pltpu.make_async_copy(src, dst, sems.new())
        copy.start()
        return copy

    my_cols = pl.ds(pl.multiple_of(x * width, width), width)
    my_rows = pl.ds(pl.multiple_of(x * rows, rows), rows)
    in_f = [load(frames.at[:, my_cols], fcols), load(len_keys, lens.at[0]), load(len_values, lens.at[1])]
    in_q = [load(frames.at[my_rows, :], frows), load(w_query, wqf.at[x])]
    in_c = [load(w_out, wof.at[x]), load(cotangent.at[my_rows, :], cot.at[:, my_cols])]
    in_k = [load(w_key, wkv.at[0]), load(w_value, wkv.at[1])]

    barrier = pltpu.get_barrier_semaphore()
    pl.semaphore_signal(barrier, inc=1, device_id=(other, x), device_id_type=MESH)
    for dx in range(1, n_x):
        pl.semaphore_signal(
            barrier, inc=1, device_id=(me, lax.rem(x + dx, n_x)), device_id_type=MESH
        )

    @pl.loop(1, n_chip)
    def _(d):
        pl.semaphore_signal(
            barrier, inc=1, device_id=(lax.rem(me + 2 * d, 2 * n_chip), x), device_id_type=MESH
        )

    pl.semaphore_wait(barrier, 1 + (n_x - 1) + (n_chip - 1))

    sent = []

    def landed(ref, sem):
        pltpu.make_async_copy(ref, ref, sem).wait()

    def to_other(src, dst):
        s, r = sems.new(), sems.new()
        pltpu.make_async_remote_copy(src, dst, s, r, device_id=(other, x), device_id_type=MESH).start()
        sent.append((src, s))
        return lambda: landed(dst, r)

    def to_x(src, dst, three):
        s, r = sems.new(), sems.new()
        for dx in (2, 1, 3):
            peer = lax.rem(x + dx, n_x)
            pltpu.make_async_remote_copy(
                src(peer), dst(n_x - dx), s, r, device_id=(me, peer), device_id_type=MESH
            ).start()
        sent.append((three, s))
        return lambda: landed(three, r)

    def to_chips(src, dst, fifteen):
        s, r = sems.new(), sems.new()

        @pl.loop(1, n_chip)
        def _(d):
            peer = lax.rem(chip + d, n_chip)
            pltpu.make_async_remote_copy(
                src(peer), dst(n_chip - d), s, r, device_id=(2 * peer + core, x), device_id_type=MESH
            ).start()

        sent.append((fifteen, s))
        return lambda: landed(fifteen, r)

    def piece(i):
        return pl.ds(pl.multiple_of(i * 16, 16), 16)

    hq = pl.ds(pl.multiple_of(core * 512, 512), 512)
    ho = pl.ds(pl.multiple_of(core * 128, 128), 128)
    got_wq = to_x(lambda p: w_query.at[hq, :], lambda o: wqf.at[x, hq, :], wqf.at[0:3, 0:512, :])
    got_cot = to_x(
        lambda p: cotangent.at[pl.ds(pl.multiple_of(p * rows, rows), rows), :],
        lambda o: cot.at[:, my_cols],
        cot.at[:, 0 : 3 * width],
    )
    got_wo = to_x(lambda p: w_out.at[ho, :], lambda o: wof.at[x, ho, :], wof.at[0:3, 0:128, :])

    for copy in in_f:
        copy.wait()

    @pl.loop(0, 2)
    def _(t):
        fpart[t] = dot(lens[t], fcols[...]).astype(BF)

    got_f = to_other(fpart.at[1 - core], fpair)

    @pl.loop(0, 2)
    def _(t):
        @pl.loop(0, 4)
        def _(b):
            at = pl.ds(pl.multiple_of(b * 512, 512), 512)
            len_t[t, at, :] = flip(lens[t, :, at])

    got_f()
    fsum[...] = (fpart[core].astype(F32) + fpair[...].astype(F32)).astype(BF)
    got_frs = to_chips(lambda j: fsum.at[piece(j), :], lambda o: frs.at[o], frs.at[1:n_chip])

    for copy in in_q + in_k:
        copy.wait()
    got_frs()
    total = fsum[piece(chip), :].astype(F32)
    for o in range(1, n_chip):
        total = total + frs[o].astype(F32)
    fx[x] = total.astype(BF)
    got_fx = to_x(lambda p: fx.at[x], lambda o: fx.at[x], fx.at[0:3])
    got_fx()
    total = dot(fx[0], wkv[core, 0:width, :])
    for b in range(1, n_x):
        total = total + dot(fx[b], wkv[core, b * width : (b + 1) * width, :])
    kpx[x] = total.astype(BF)
    got_kpx = to_x(lambda p: kpx.at[x], lambda o: kpx.at[x], kpx.at[0:3])

    def gather(src, full, fifteen):
        copy = load(src, full(core, chip))
        done = to_chips(lambda j: src, lambda o: full(core, chip), fifteen)

        def arrive():
            copy.wait()
            done()

        return arrive

    got_kpx()
    got_kvp = gather(kpx, lambda t, j: kvp.at[t, :, piece(j), :], kvp.at[0, :, 0:240, :])
    got_ff = gather(fx, lambda t, j: ff.at[t, :, piece(j), :], ff.at[0, :, 0:240, :])

    got_wq()
    s, r_wq = sems.new(), sems.new()
    for dx in range(1, n_x):
        b = lax.rem(x + dx, n_x)
        pltpu.make_async_remote_copy(
            wqf.at[b, hq, :], wqf.at[b, hq, :], s, r_wq, device_id=(other, x), device_id_type=MESH
        ).start()
    sent.append((wqf.at[0:3, 0:512, :], s))
    landed(wqf.at[0:3, 0:512, :], r_wq)

    @pl.loop(0, n_x)
    def _(g):
        q[g] = dot(frows[...], wqf[g]).astype(BF)

    got_kvp()
    got_kvo = to_other(kvp.at[core], kvp.at[core])
    got_wo()
    s, r_wo = sems.new(), sems.new()
    for dx in range(1, n_x):
        b = lax.rem(x + dx, n_x)
        pltpu.make_async_remote_copy(
            wof.at[b, ho, :], wof.at[b, ho, :], s, r_wo, device_id=(other, x), device_id_type=MESH
        ).start()
    sent.append((wof.at[0:3, 0:128, :], s))
    landed(wof.at[0:3, 0:128, :], r_wo)
    for copy in in_c:
        copy.wait()
    got_cot()

    @pl.loop(0, n_x)
    def _(g):
        ga[g] = dot_nt(cot[...], wof[g]).astype(BF)

    got_ff()
    got_ffo = to_other(ff.at[core], ff.at[core])
    got_kvo()

    lane = lax.broadcasted_iota(jnp.int32, (width, width), 1) // DH

    def only(h, a):
        return jnp.where(lane == h, a.astype(F32), 0.0).astype(BF)

    @pl.loop(0, n_x)
    def _(g):
        kg = kvp[0, g]
        vg_t = flip(kvp[1, g])
        qg = q[g]
        for h in range(4):
            scores = dot_nt(only(h, kg), qg)
            top = jnp.max(scores, axis=0, keepdims=True)
            e = jnp.exp((scores - top) * (DH ** -0.5))
            p = (e * (1.0 / jnp.sum(e, axis=0, keepdims=True))).astype(BF)
            prob[4 * g + h] = p
            att_t[g, h * DH : (h + 1) * DH, :] = dot(vg_t[h * DH : (h + 1) * DH, :], p).astype(BF)
        att[g] = flip(att_t[g])

    @pl.loop(0, n_x)
    def _(n):
        at = pl.ds(pl.multiple_of(n * width, width), width)
        total = dot(att[0], wof[0, :, at])
        for g in range(1, n_x):
            total = total + dot(att[g], wof[g, :, at])
        mix_s[n] = total.astype(BF)

    got_mix = to_x(
        lambda p: mix_s.at[p], lambda o: mix_r.at[my_rows, :], mix_r.at[0 : 3 * rows, :]
    )
    own_mix = load(mix_s.at[x], mix_r.at[my_rows, :])

    half = w_pair.shape[-1]
    mine = pl.ds(pl.multiple_of(core * half, half), half)
    theirs = pl.ds(pl.multiple_of((1 - core) * half, half), half)

    @pl.loop(0, n_x)
    def _(g):
        w_s[0, g] = dot(att_t[g], cot[...]).astype(BF)

    got_wpair = [to_other(w_s.at[0, :, :, theirs], w_pair.at[0])]

    @pl.loop(0, n_x)
    def _(g):
        vg = kvp[1, g]
        kg_t = flip(kvp[0, g])
        qg = q[g]
        gag = ga[g]
        gk = jnp.zeros((width, width), F32)
        gv = jnp.zeros((width, width), F32)
        for h in range(4):
            pb = prob[4 * g + h]
            p = pb.astype(F32)
            gp = dot_nt(only(h, vg), gag)
            inner = jnp.sum(p * gp, axis=0, keepdims=True)
            gs = (p * (gp - inner) * (DH ** -0.5)).astype(BF)
            gq_t[g, h * DH : (h + 1) * DH, :] = dot(kg_t[h * DH : (h + 1) * DH, :], gs).astype(BF)
            gk = jnp.where(lane == h, dot(gs, qg), gk)
            gv = jnp.where(lane == h, dot(pb, gag), gv)
        gkv[0, g] = gk.astype(BF)
        gkv[1, g] = gv.astype(BF)
        gq[g] = flip(gq_t[g])

    got_gpair = to_other(gkv.at[1 - core], gkv_pair)

    def pair_sum(k):
        got_wpair[k]()

        @pl.loop(0, n_x)
        def _(g):
            w_sum[k, g] = (w_s[k, g, :, mine].astype(F32) + w_pair[k, g].astype(F32)).astype(BF)

        return to_chips(
            lambda j: w_sum.at[k, :, piece(j), :], lambda o: w_rs.at[k, o], w_rs.at[k, 1:n_chip]
        )

    @pl.loop(0, n_x)
    def _(n):
        at = pl.ds(pl.multiple_of(n * width, width), width)
        total = dot_nt(gq[0], wqf[0, at, :])
        for g in range(1, n_x):
            total = total + dot_nt(gq[g], wqf[g, at, :])
        gf_s[n] = total.astype(BF)

    got_gf = to_x(lambda p: gf_s.at[p], lambda o: gf_r.at[my_rows, :], gf_r.at[0 : 3 * rows, :])
    own_gf = load(gf_s.at[x], gf_r.at[my_rows, :])

    got_gpair()

    @pl.loop(0, n_x)
    def _(g):
        gkv_sum[g] = (gkv[core, g].astype(F32) + gkv_pair[g].astype(F32)).astype(BF)

    got_grs = to_chips(lambda j: gkv_sum.at[:, piece(j), :], lambda o: gkv_rs.at[o], gkv_rs.at[1:n_chip])

    @pl.loop(0, n_x)
    def _(g):
        w_s[1, g] = dot(gq_t[g], frows[...]).astype(BF)

    got_wpair.append(to_other(w_s.at[1, :, :, theirs], w_pair.at[1]))
    got_wrs = [pair_sum(0)]

    got_grs()
    total = gkv_sum[:, piece(chip), :].astype(F32)
    for o in range(1, n_chip):
        total = total + gkv_rs[o].astype(F32)
    gkv_x[...] = total.astype(BF)
    got_gx = to_x(lambda p: gkv_x.at[p], lambda o: gkv_xr.at[o], gkv_xr.at[1:n_x])
    got_wrs.append(pair_sum(1))
    got_gx()
    total = gkv_x[x].astype(F32)
    for o in range(1, n_x):
        total = total + gkv_xr[o].astype(F32)
    g16 = total.astype(BF)
    gk16[0] = g16
    for n in range(n_x):
        m_s[n] = dot_nt(g16, wkv[core, n * width : (n + 1) * width, :]).astype(BF)
    got_m = to_x(lambda p: m_s.at[p], lambda o: m_r.at[o], m_r.at[1:n_x])

    def over_x(k):
        got_wrs[k]()
        total = w_sum[k, :, piece(chip), :].astype(F32)
        for o in range(1, n_chip):
            total = total + w_rs[k, o].astype(F32)
        w_x[k] = total.astype(BF)
        return to_x(lambda p: w_x.at[k, p], lambda o: w_xr.at[k, o], w_xr.at[k, 1:n_x])

    got_m()
    total = m_s[x].astype(F32)
    for o in range(1, n_x):
        total = total + m_r[o].astype(F32)
    gk16[1] = total.astype(BF)
    got_gkm = gather(gk16, lambda t, j: gkm.at[t, :, piece(j), :], gkm.at[0, :, 0:240, :])

    got_wx = [over_x(0)]
    got_wx.append(over_x(1))

    def gather_w(k):
        got_wx[k]()
        total = w_x[k, x].astype(F32)
        for o in range(1, n_x):
            total = total + w_xr[k, o].astype(F32)
        w_f[k] = total.astype(BF)
        return gather(w_f.at[k], lambda t, j: w_ag.at[k, t, piece(j), :], w_ag.at[k, 0, 0:240, :])

    got_ffo()
    got_gkm()
    got_gkmo = to_other(gkm.at[core], gkm.at[core])
    got_w = [gather_w(0)]
    got_w.append(gather_w(1))
    outs = []
    own_mix.wait()
    got_mix()
    outs.append(load(mix_r, mixed_o))
    own_gf.wait()
    got_gf()
    got_gkmo()

    @pl.loop(0, n_x)
    def _(b):
        at = pl.ds(pl.multiple_of(b * rows, rows), rows)
        total = gf_r[at, :].astype(F32) + dot(len_t[0, at, :], gkm[0, 1]) + dot(len_t[1, at, :], gkm[1, 1])
        gf_r[at, :] = total.astype(BF)

    outs.append(load(gf_r, gframes_o))
    got_wo2 = []
    for k in range(2):
        got_w[k]()
        got_wo2.append(to_other(w_ag.at[k, core], w_ag.at[k, core]))

    @pl.loop(0, n_x)
    def _(g):
        at = pl.ds(pl.multiple_of(g * width, width), width)
        gwk_o[at, :] = dot(flip(ff[0, g]), gkm[0, 0])
        gwv_o[at, :] = dot(flip(ff[1, g]), gkm[1, 0])

    got_wo2[0]()
    for t in range(2):
        gwo_o[:, t * half : (t + 1) * half] = w_ag[0, t].astype(F32)
    got_wo2[1]()
    for t in range(2):
        gwq_o[t * half : (t + 1) * half, :] = w_ag[1, t].astype(F32).T
    for ref, sem in sent:
        landed(ref, sem)
    for copy in outs:
        copy.wait()


def body(frames, len_keys, len_values, w_query, w_key, w_value, w_out, cotangent):
    span, depth = frames.shape
    rows = span // 4
    bf = lambda *shape: pltpu.VMEM(shape, BF)
    scratch = [
        bf(span, 256), bf(rows, depth), bf(2, 256, span), bf(2, span, 256),
        bf(4, 1024, 256), bf(4, 256, 1024), bf(2, 1024, 256), bf(rows, depth),
        bf(2, 256, 256), bf(256, 256), bf(256, 256), bf(16, 16, 256),
        bf(4, 16, 256), bf(4, 16, 256), bf(2, 4, 256, 256), bf(2, 4, 256, 256),
        bf(4, rows, 256), bf(4, rows, 256), bf(16, 256, rows),
        bf(4, 256, rows), bf(4, rows, 256), bf(4, 256, rows), bf(4, rows, 256),
        bf(4, rows, 256), bf(span, 256), bf(4, rows, 256), bf(span, 256),
        bf(2, 4, 256, 256), bf(4, 256, 256), bf(4, 256, 256), bf(16, 4, 16, 256),
        bf(4, 16, 256), bf(4, 16, 256), bf(2, 16, 256), bf(4, 16, 256), bf(4, 16, 256),
        bf(2, 2, 256, 256),
        bf(2, 4, 256, 1024), bf(2, 4, 256, 512), bf(2, 4, 256, 512), bf(2, 16, 4, 16, 512),
        bf(2, 4, 16, 512), bf(2, 4, 16, 512), bf(2, 2, 256, 512), bf(2, 16, 512),
        pltpu.SemaphoreType.DMA((80,)),
    ]
    any_ = pl.BlockSpec(memory_space=pl.ANY)
    vm = pl.BlockSpec(memory_space=pltpu.VMEM)
    return pl.pallas_call(
        kernel,
        out_shape=(
            jax.ShapeDtypeStruct((span, 256), BF),
            jax.ShapeDtypeStruct((span, 256), BF),
            jax.ShapeDtypeStruct((depth, 256), F32),
            jax.ShapeDtypeStruct((depth, 256), F32),
            jax.ShapeDtypeStruct((depth, 256), F32),
            jax.ShapeDtypeStruct((256, depth), F32),
        ),
        in_specs=[any_] * 8,
        out_specs=(any_, any_, vm, vm, vm, vm),
        scratch_shapes=scratch,
        compiler_params=pltpu.CompilerParams(
            collective_id=0, has_side_effects=True, vmem_limit_bytes=60 * 1024 * 1024
        ),
        cost_estimate=pl.CostEstimate(flops=14_000_000_000, bytes_accessed=24_000_000, transcendentals=2_097_152),
    )(frames, len_keys, len_values, w_query, w_key, w_value, w_out, cotangent)


def solution(mesh):
    placed = (
        P("ctx", None),
        P(None, "ctx"),
        P(None, "ctx"),
        P(None, "head"),
        P(None, "head"),
        P(None, "head"),
        P("head", None),
        P("ctx", "head"),
    )
    return jax.shard_map(
        body,
        mesh=mesh,
        in_specs=placed,
        out_specs=(
            P("ctx", "head"),
            P("ctx", "head"),
            P(None, "head"),
            P(None, "head"),
            P(None, "head"),
            P("head", None),
        ),
        check_vma=False,
    )
```

```python
import jax
import jax.numpy as jnp
from jax import lax
from jax.experimental import pallas as pl
from jax.experimental.pallas import tpu as pltpu
from jax.sharding import PartitionSpec as P

DH = 64
SCALE = DH ** -0.5
N_X = 4
N_CHIP = 16
WIDTH = 256
HALF = 512
MESH = pl.DeviceIdType.MESH
BF = jnp.bfloat16
F32 = jnp.float32


def dot(a, b):
    return jnp.dot(a, b, preferred_element_type=F32)


def dot_nt(a, b):
    return lax.dot_general(a, b, (((1,), (1,)), ((), ())), preferred_element_type=F32)


def flip(a):
    return a.astype(F32).T.astype(BF)


class Sems:
    def __init__(self, ref):
        self.ref, self.used = ref, 0

    def new(self):
        self.used += 1
        return self.ref.at[self.used - 1]


def kernel(
    frames, len_keys, len_values, w_query, w_key, w_value, w_out, cotangent,
    mixed_o, gframes_o, gwk_o, gwv_o, gw_o,
    fcols, frows, lens, len_t, wqf, wof, wo_p, wkv, cot,
    fpart, fpair, fsum, frs, fx, kpx, ff, kvp,
    q, ga, prob, att_t, att, gq_t, gq,
    mix_s, mix_r, gf_s, gf_r,
    gkv, gkv_pair, gkv_sum, gkv_rs, gkv_x, gkv_xr, gk16, m_s, m_r, gkm,
    w_s, w_pair, w_sum, w_ra, w_s2, w_rb, w_x, w_xr, w_f, w_ag, gwk_v, gwv_v, sem_ref,
):
    sems = Sems(sem_ref)
    me = lax.axis_index("ctx")
    x = lax.axis_index("head")
    core = lax.rem(me, 2)
    chip = lax.div(me, 2)
    other = me + 1 - 2 * core
    rows = frows.shape[0]
    step_a = 1 + 3 * core
    step_b = 4 - 3 * core
    at_a = lax.rem(lax.div(chip, step_a), N_X)
    at_b = lax.rem(lax.div(chip, step_b), N_X)

    def block(i, size):
        return pl.ds(pl.multiple_of(i * size, size), size)

    def beyond(o):
        return lax.rem(x + o, N_X)

    def piece(i):
        return block(i, 16)

    my_cols = block(x, WIDTH)
    my_rows = block(x, rows)
    mine = block(core, HALF)
    theirs = block(1 - core, HALF)
    hq = block(core, HALF)

    def load(src, dst):
        copy = pltpu.make_async_copy(src, dst, sems.new())
        copy.start()
        return copy

    in_f = [load(frames.at[:, my_cols], fcols), load(len_keys, lens.at[0]), load(len_values, lens.at[1])]
    in_w = [load(w_out.at[piece(chip), mine], wo_p.at[0])]
    in_k = [load(w_key, wkv.at[0]), load(w_value, wkv.at[1])]
    in_q = [load(frames.at[my_rows, :], frows), load(w_query, wqf.at[0])]
    in_c = [load(cotangent.at[my_rows, :], cot.at[:, my_cols])]

    barrier = pltpu.get_barrier_semaphore()
    pl.semaphore_signal(barrier, inc=1, device_id=(other, x), device_id_type=MESH)
    for dx in range(1, N_X):
        pl.semaphore_signal(barrier, inc=1, device_id=(me, beyond(dx)), device_id_type=MESH)

    @pl.loop(1, N_CHIP)
    def _(d):
        pl.semaphore_signal(
            barrier, inc=1, device_id=(lax.rem(me + 2 * d, 2 * N_CHIP), x), device_id_type=MESH
        )

    for copy in in_f:
        copy.wait()

    @pl.loop(0, 2)
    def _(t):
        fpart[t] = dot(lens[t], fcols[...]).astype(BF)

    pl.semaphore_wait(barrier, 1 + (N_X - 1) + (N_CHIP - 1))

    sent = []

    def landed(ref, sem):
        pltpu.make_async_copy(ref, ref, sem).wait()

    def remote(src, dst, s, r, device):
        pltpu.make_async_remote_copy(src, dst, s, r, device_id=device, device_id_type=MESH).start()

    def to_other(pairs, whole):
        s, r = sems.new(), sems.new()
        for src, dst in pairs:
            remote(src, dst, s, r, (other, x))
        sent.append((whole, s))
        return lambda: landed(whole, r)

    def to_x(src, dst, whole, which=(1, 3, 2)):
        s, r = sems.new(), sems.new()
        for dx in which:
            remote(src(dx), dst(N_X - dx), s, r, (me, beyond(dx)))
        sent.append((whole, s))
        return lambda: landed(whole, r)

    def to_chips(src, dst, whole):
        s, r = sems.new(), sems.new()

        @pl.loop(1, N_CHIP)
        def _(d):
            peer = lax.rem(chip + d, N_CHIP)
            remote(src(peer), dst(N_CHIP - d), s, r, (2 * peer + core, x))

        sent.append((whole, s))
        return lambda: landed(whole, r)

    def to_line(src, dst, whole, at, step):
        s, r = sems.new(), sems.new()
        for d in (1, 3, 2):
            peer = lax.rem(at + d, N_X)
            remote(src(peer), dst(N_X - d), s, r, (me + 2 * step * (peer - at), x))
        sent.append((whole, s))
        return lambda: landed(whole, r)

    def gather(src, full, fifteen):
        copy = load(src, full)
        done = to_chips(lambda j: src, lambda o: full, fifteen)

        def arrive():
            copy.wait()
            done()

        return arrive

    def add(first, slots, count):
        total = first.astype(F32)
        for o in range(1, count):
            total = total + slots(o).astype(F32)
        return total.astype(BF)

    got_f = to_other([(fpart.at[1 - core], fpair)], fpair)
    got_wo = to_x(lambda dx: w_out.at[piece(chip), mine], lambda o: wo_p.at[o], wo_p.at[1:N_X])
    got_wq = to_x(
        lambda dx: w_query.at[hq, :], lambda o: wqf.at[o, hq, :], wqf.at[0:2, 0:HALF, :], (1, 3)
    )

    @pl.loop(0, 2)
    def _(t):
        @pl.loop(0, 4)
        def _(b):
            at = block(b, 512)
            len_t[t, at, :] = flip(lens[t, :, at])

    got_f()
    fsum[...] = (fpart[core].astype(F32) + fpair[...].astype(F32)).astype(BF)
    got_frs = to_chips(lambda j: fsum.at[piece(j), :], lambda o: frs.at[o], frs.at[1:N_CHIP])
    for copy in in_w:
        copy.wait()
    got_wo()
    got_wof = gather(wo_p, wof.at[:, piece(chip), mine], wof.at[:, 0:240, 0:HALF])
    for copy in in_k + in_q:
        copy.wait()
    got_frs()
    fx[0] = add(fsum[piece(chip), :], lambda o: frs[o], N_CHIP)
    got_fx = to_x(lambda dx: fx.at[0], lambda o: fx.at[o], fx.at[1:N_X])
    q[0] = dot(frows[...], wqf[0]).astype(BF)
    got_fx()
    total = dot(fx[0], wkv[core, my_cols, :])
    for o in range(1, N_X):
        total = total + dot(fx[o], wkv[core, block(beyond(o), WIDTH), :])
    kpx[0] = total.astype(BF)
    got_kpx = to_x(lambda dx: kpx.at[0], lambda o: kpx.at[o], kpx.at[1:N_X])
    got_wq2 = to_x(lambda dx: w_query.at[hq, :], lambda o: wqf.at[o, hq, :], wqf.at[0, 0:HALF, :], (2,))
    got_cot = to_x(
        lambda dx: cotangent.at[block(beyond(dx), rows), :],
        lambda o: cot.at[:, my_cols],
        cot.at[:, 0 : 3 * WIDTH],
    )
    got_kpx()
    got_kvp = gather(kpx, kvp.at[core, :, piece(chip), :], kvp.at[0, :, 0:240, :])

    got_wq()
    got_wqo = to_other([(wqf.at[o, hq, :], wqf.at[o, hq, :]) for o in (1, 3)], wqf.at[0:2, 0:HALF, :])
    got_wqo()
    for o in (1, 3):
        q[o] = dot(frows[...], wqf[o]).astype(BF)
    got_wof()
    got_woo = to_other([(wof.at[:, :, mine], wof.at[:, :, mine])], wof.at[:, :, 0:HALF])
    got_kvp()
    got_kvo = to_other([(kvp.at[core], kvp.at[core])], kvp.at[0])
    got_ff = gather(fx, ff.at[core, :, piece(chip), :], ff.at[0, :, 0:240, :])
    got_wq2()
    got_wqo2 = to_other([(wqf.at[2, hq, :], wqf.at[2, hq, :])], wqf.at[0, 0:HALF, :])
    got_wqo2()
    q[2] = dot(frows[...], wqf[2]).astype(BF)
    got_kvo()

    lane = lax.broadcasted_iota(jnp.int32, (WIDTH, WIDTH), 1) // DH

    def only(h, a):
        return jnp.where(lane == h, a.astype(F32), 0.0).astype(BF)

    @pl.loop(0, N_X)
    def _(g):
        kg = kvp[0, g]
        vg_t = flip(kvp[1, g])
        qg = q[g]
        for h in range(4):
            scores = dot_nt(only(h, kg), qg)
            top = jnp.max(scores, axis=0, keepdims=True)
            e = jnp.exp((scores - top) * SCALE)
            p = (e * (1.0 / jnp.sum(e, axis=0, keepdims=True))).astype(BF)
            prob[4 * g + h] = p
            att_t[g, h * DH : (h + 1) * DH, :] = dot(vg_t[h * DH : (h + 1) * DH, :], p).astype(BF)
        att[g] = flip(att_t[g])

    got_woo()

    @pl.loop(0, N_X)
    def _(n):
        at = block(beyond(n), WIDTH)
        heads = jnp.concatenate([att[o] for o in range(N_X)], axis=1)
        weights = jnp.concatenate([wof[o, :, at] for o in range(N_X)], axis=0)
        mix_s[n] = dot(heads, weights).astype(BF)

    got_mix = to_x(lambda dx: mix_s.at[dx], lambda o: mix_r.at[my_rows, :], mix_r.at[0 : 3 * rows, :])
    own_mix = load(mix_s.at[0], mix_r.at[my_rows, :])

    for copy in in_c:
        copy.wait()
    got_cot()

    @pl.loop(0, N_X)
    def _(g):
        w_s[0, g] = dot(att_t[g], cot[...]).astype(BF)

    got_wpair = [to_other([(w_s.at[0, :, :, theirs], w_pair.at[0])], w_pair.at[0])]

    @pl.loop(0, N_X)
    def _(g):
        ga[g] = dot_nt(cot[...], wof[g]).astype(BF)

    def stage_a(k):
        got_wpair[k]()

        @pl.loop(0, N_X)
        def _(g):
            w_sum[k, g] = (w_s[k, g, :, mine].astype(F32) + w_pair[k, g].astype(F32)).astype(BF)

        return to_line(
            lambda p: w_sum.at[k, :, block(p, 64), :], lambda o: w_ra.at[k, o], w_ra.at[k, 1:N_X], at_a, step_a
        )

    def stage_b(k):
        got_wa[k]()

        @pl.loop(0, N_X)
        def _(g):
            w_s2[k, g] = add(w_sum[k, g, block(at_a, 64), :], lambda o: w_ra[k, o, g], N_X)

        return to_line(
            lambda p: w_s2.at[k, :, piece(p), :], lambda o: w_rb.at[k, o], w_rb.at[k, 1:N_X], at_b, step_b
        )

    def stage_x(k):
        got_wb[k]()
        w_x[k] = add(w_s2[k, :, piece(at_b), :], lambda o: w_rb[k, o], N_X)
        return to_x(lambda dx: w_x.at[k, dx], lambda o: w_xr.at[k, o], w_xr.at[k, 1:N_X])

    def stage_w(k):
        got_wx[k]()
        w_f[k] = add(w_x[k, 0], lambda o: w_xr[k, o], N_X)
        return gather(w_f.at[k], w_ag.at[k, core, piece(4 * at_a + at_b), :], w_ag.at[k, 0, 0:240, :])

    got_wa = [stage_a(0)]
    got_ff()
    got_ffo = to_other([(ff.at[core], ff.at[core])], ff.at[0])

    def backward(g):
        vg = kvp[1, g]
        kg_t = flip(kvp[0, g])
        qg = q[g]
        gag = ga[g]
        gk = jnp.zeros((WIDTH, WIDTH), F32)
        gv = jnp.zeros((WIDTH, WIDTH), F32)
        for h in range(4):
            pb = prob[4 * g + h]
            p = pb.astype(F32)
            gp = dot_nt(only(h, vg), gag)
            inner = jnp.sum(p * gp, axis=0, keepdims=True)
            gs = (p * (gp - inner) * SCALE).astype(BF)
            gq_t[g, h * DH : (h + 1) * DH, :] = dot(kg_t[h * DH : (h + 1) * DH, :], gs).astype(BF)
            gk = jnp.where(lane == h, dot(gs, qg), gk)
            gv = jnp.where(lane == h, dot(pb, gag), gv)
        gkv[0, g] = gk.astype(BF)
        gkv[1, g] = gv.astype(BF)
        gq[g] = flip(gq_t[g])

    pl.loop(0, 3)(backward)
    got_wb = [stage_b(0)]
    pl.loop(3, N_X)(backward)

    got_gpair = to_other([(gkv.at[1 - core], gkv_pair)], gkv_pair)

    @pl.loop(0, N_X)
    def _(g):
        w_s[1, g] = dot(gq_t[g], frows[...]).astype(BF)

    got_wpair.append(to_other([(w_s.at[1, :, :, theirs], w_pair.at[1])], w_pair.at[1]))
    got_gpair()

    @pl.loop(0, N_X)
    def _(g):
        gkv_sum[g] = (gkv[core, g].astype(F32) + gkv_pair[g].astype(F32)).astype(BF)

    got_grs = to_chips(lambda j: gkv_sum.at[:, piece(j), :], lambda o: gkv_rs.at[o], gkv_rs.at[1:N_CHIP])
    got_wx = [stage_x(0)]
    got_wa.append(stage_a(1))

    @pl.loop(0, N_X)
    def _(n):
        at = block(beyond(n), WIDTH)
        heads = jnp.concatenate([gq[o] for o in range(N_X)], axis=1)
        weights = jnp.concatenate([wqf[o, at, :] for o in range(N_X)], axis=1)
        gf_s[n] = dot_nt(heads, weights).astype(BF)

    def send_gf(which):
        return to_x(
            lambda dx: gf_s.at[dx], lambda o: gf_r.at[my_rows, :], gf_r.at[0 : len(which) * rows, :], which
        )

    got_gf = [send_gf((1, 3))]
    own_gf = load(gf_s.at[0], gf_r.at[my_rows, :])

    got_grs()
    gkv_x[...] = add(gkv_sum[:, piece(chip), :], lambda o: gkv_rs[o], N_CHIP)
    got_gx = to_x(lambda dx: gkv_x.at[dx], lambda o: gkv_xr.at[o], gkv_xr.at[1:N_X])
    got_w = [stage_w(0)]
    got_gx()
    gk16[0] = add(gkv_x[0], lambda o: gkv_xr[o], N_X)
    for o in range(N_X):
        m_s[o] = dot_nt(gk16[0], wkv[core, block(beyond(o), WIDTH), :]).astype(BF)
    got_m = to_x(lambda dx: m_s.at[dx], lambda o: m_r.at[o], m_r.at[1:N_X])
    got_gf.append(send_gf((2,)))
    got_m()
    gk16[1] = add(m_s[0], lambda o: m_r[o], N_X)
    got_gkm = gather(gk16, gkm.at[core, :, piece(chip), :], gkm.at[0, :, 0:240, :])
    got_wb.append(stage_b(1))
    got_w[0]()
    got_wo2 = [to_other([(w_ag.at[0, core], w_ag.at[0, core])], w_ag.at[0, 0])]
    outs = []
    own_mix.wait()
    got_mix()
    outs.append(load(mix_r, mixed_o))
    got_wx.append(stage_x(1))
    got_gkm()
    got_gkmo = to_other([(gkm.at[core], gkm.at[core])], gkm.at[0])
    got_w.append(stage_w(1))
    got_ffo()
    got_gkmo()

    @pl.loop(0, N_X)
    def _(o):
        at = block(beyond(o), WIDTH)
        gwk_v[at, :] = dot(flip(ff[0, o]), gkm[0, 0]).astype(BF)
        gwv_v[at, :] = dot(flip(ff[1, o]), gkm[1, 0]).astype(BF)

    outs.append(load(gwk_v, gwk_o))
    outs.append(load(gwv_v, gwv_o))
    own_gf.wait()
    for wait in got_gf:
        wait()

    @pl.loop(0, N_X)
    def _(b):
        at = block(b, rows)
        total = gf_r[at, :].astype(F32) + dot(len_t[0, at, :], gkm[0, 1]) + dot(len_t[1, at, :], gkm[1, 1])
        gf_r[at, :] = total.astype(BF)

    outs.append(load(gf_r, gframes_o))
    got_wo2[0]()
    outs.append(load(w_ag.at[0], gw_o.at[0]))
    got_w[1]()
    got_wo2.append(to_other([(w_ag.at[1, core], w_ag.at[1, core])], w_ag.at[1, 0]))
    got_wo2[1]()
    outs.append(load(w_ag.at[1], gw_o.at[1]))
    for ref, sem in sent:
        landed(ref, sem)
    for copy in outs:
        copy.wait()


def finish(
    mixed, gframes, gwk, gwv, gw,
    mixed_o, gframes_o, gwq_o, gwk_o, gwv_o, gwo_o,
    raw_k, raw_w, raw_f, wide, wide_o, sem_ref,
):
    sems = Sems(sem_ref)

    def copy(src, dst):
        c = pltpu.make_async_copy(src, dst, sems.new())
        c.start()
        return c

    ins = [copy(gwk, raw_k.at[0]), copy(gwv, raw_k.at[1]), copy(gw.at[0], raw_w.at[0]), copy(gw.at[1], raw_w.at[1])]
    through = [copy(mixed, raw_f.at[0]), copy(gframes, raw_f.at[1])]
    outs = []
    for k, out in enumerate((gwk_o, gwv_o)):
        ins[k].wait()
        wide[k] = raw_k[k].astype(F32)
        outs.append(copy(wide.at[k], out))
    for k, out in enumerate((mixed_o, gframes_o)):
        through[k].wait()
        outs.append(copy(raw_f.at[k], out))
    ins[2].wait()
    for t in range(2):
        wide_o[:, t * HALF : (t + 1) * HALF] = raw_w[0, t].astype(F32)
    outs.append(copy(wide_o, gwo_o))
    ins[3].wait()
    for t in range(2):
        wide[2, t * HALF : (t + 1) * HALF, :] = raw_w[1, t].astype(F32).T
    outs.append(copy(wide.at[2], gwq_o))
    for c in outs:
        c.wait()


def body(frames, len_keys, len_values, w_query, w_key, w_value, w_out, cotangent):
    span, depth = frames.shape
    rows = span // N_X

    def bf(*shape):
        return pltpu.VMEM(shape, BF)

    scratch = [
        bf(span, 256), bf(rows, depth), bf(2, 256, span), bf(2, span, 256),
        bf(4, 1024, 256), bf(4, 256, 1024), bf(4, 16, 512), bf(2, 1024, 256), bf(rows, depth),
        bf(2, 256, 256), bf(256, 256), bf(256, 256), bf(16, 16, 256),
        bf(4, 16, 256), bf(4, 16, 256), bf(2, 4, 256, 256), bf(2, 4, 256, 256),
        bf(4, rows, 256), bf(4, rows, 256), bf(16, 256, rows),
        bf(4, 256, rows), bf(4, rows, 256), bf(4, 256, rows), bf(4, rows, 256),
        bf(4, rows, 256), bf(span, 256), bf(4, rows, 256), bf(span, 256),
        bf(2, 4, 256, 256), bf(4, 256, 256), bf(4, 256, 256), bf(16, 4, 16, 256),
        bf(4, 16, 256), bf(4, 16, 256), bf(2, 16, 256), bf(4, 16, 256), bf(4, 16, 256),
        bf(2, 2, 256, 256),
        bf(2, 4, 256, 1024), bf(2, 4, 256, 512), bf(2, 4, 256, 512), bf(2, 4, 4, 64, 512),
        bf(2, 4, 64, 512), bf(2, 4, 4, 16, 512), bf(2, 4, 16, 512), bf(2, 4, 16, 512),
        bf(2, 16, 512), bf(2, 2, 256, 512), bf(depth, 256), bf(depth, 256),
        pltpu.SemaphoreType.DMA((100,)),
    ]
    any_ = pl.BlockSpec(memory_space=pl.ANY)
    shape = jax.ShapeDtypeStruct
    raw = pl.pallas_call(
        kernel,
        out_shape=(
            shape((span, 256), BF), shape((span, 256), BF),
            shape((depth, 256), BF), shape((depth, 256), BF), shape((2, 2, 256, 512), BF),
        ),
        in_specs=[any_] * 8,
        out_specs=(any_,) * 5,
        scratch_shapes=scratch,
        compiler_params=pltpu.CompilerParams(
            collective_id=0, has_side_effects=True, vmem_limit_bytes=60 * 1024 * 1024
        ),
        cost_estimate=pl.CostEstimate(flops=14_000_000_000, bytes_accessed=24_000_000, transcendentals=2_097_152),
    )(frames, len_keys, len_values, w_query, w_key, w_value, w_out, cotangent)
    return pl.pallas_call(
        finish,
        out_shape=(
            shape((span, 256), BF), shape((span, 256), BF),
            shape((depth, 256), F32), shape((depth, 256), F32), shape((depth, 256), F32), shape((256, depth), F32),
        ),
        in_specs=[any_] * 5,
        out_specs=(any_,) * 6,
        scratch_shapes=[
            bf(2, depth, 256), bf(2, 2, 256, 512), bf(2, span, 256),
            pltpu.VMEM((3, depth, 256), F32), pltpu.VMEM((256, depth), F32),
            pltpu.SemaphoreType.DMA((12,)),
        ],
        compiler_params=pltpu.CompilerParams(vmem_limit_bytes=60 * 1024 * 1024),
        cost_estimate=pl.CostEstimate(flops=1_000_000, bytes_accessed=11_000_000, transcendentals=0),
    )(*raw)


def solution(mesh):
    placed = (
        P("ctx", None),
        P(None, "ctx"),
        P(None, "ctx"),
        P(None, "head"),
        P(None, "head"),
        P(None, "head"),
        P("head", None),
        P("ctx", "head"),
    )
    return jax.shard_map(
        body,
        mesh=mesh,
        in_specs=placed,
        out_specs=(
            P("ctx", "head"),
            P("ctx", "head"),
            P(None, "head"),
            P(None, "head"),
            P(None, "head"),
            P("head", None),
        ),
        check_vma=False,
    )
```

```python
import jax
import jax.numpy as jnp
from jax import lax
from jax.experimental import pallas as pl
from jax.experimental.pallas import tpu as pltpu
from jax.sharding import PartitionSpec as P

DH = 64
SCALE = DH ** -0.5
N_X = 4
N_CHIP = 16
WIDTH = 256
HALF = 512
MESH = pl.DeviceIdType.MESH
BF = jnp.bfloat16
F32 = jnp.float32


def dot(a, b):
    return jnp.dot(a, b, preferred_element_type=F32)


def dot_nt(a, b):
    return lax.dot_general(a, b, (((1,), (1,)), ((), ())), preferred_element_type=F32)


def flip(a):
    return a.astype(F32).T.astype(BF)


class Sems:
    def __init__(self, ref):
        self.ref, self.used = ref, 0

    def new(self):
        self.used += 1
        return self.ref.at[self.used - 1]


def kernel(
    frames, len_keys, len_values, w_query, w_key, w_value, w_out, cotangent,
    mixed_o, gframes_o, gwk_o, gwv_o, gw_o,
    fcols, frows, lens, len_t, wqf, wof, wo_p, wkv, cot,
    fpart, fpair, fsum, frs, fx, kpx, ff, kvp,
    q, ga, prob, att_t, att, gq_t, gq,
    mix_s, mix_r, gf_s, gf_r,
    gkv, gkv_pair, gkv_sum, gkv_rs, gkv_x, gkv_xr, gk16, m_s, m_r, gkm,
    w_s, w_pair, w_sum, w_ra, w_s2, w_rb, w_x, w_xr, w_f, w_ag, gwk_v, gwv_v, sem_ref,
):
    sems = Sems(sem_ref)
    me = lax.axis_index("ctx")
    x = lax.axis_index("head")
    core = lax.rem(me, 2)
    chip = lax.div(me, 2)
    other = me + 1 - 2 * core
    rows = frows.shape[0]
    step_a = 1 + 3 * core
    step_b = 4 - 3 * core
    at_a = lax.rem(lax.div(chip, step_a), N_X)
    at_b = lax.rem(lax.div(chip, step_b), N_X)

    def block(i, size):
        return pl.ds(pl.multiple_of(i * size, size), size)

    def beyond(o):
        return lax.rem(x + o, N_X)

    def piece(i):
        return block(i, 16)

    my_cols = block(x, WIDTH)
    my_rows = block(x, rows)
    mine = block(core, HALF)
    theirs = block(1 - core, HALF)
    hq = block(core, HALF)

    def load(src, dst):
        copy = pltpu.make_async_copy(src, dst, sems.new())
        copy.start()
        return copy

    in_f = [load(frames.at[:, my_cols], fcols), load(len_keys, lens.at[0]), load(len_values, lens.at[1])]
    in_w = [load(w_out.at[piece(chip), mine], wo_p.at[0])]
    in_k = [load(w_key, wkv.at[0]), load(w_value, wkv.at[1])]
    in_q = [load(frames.at[my_rows, :], frows), load(w_query, wqf.at[0])]
    in_c = [load(cotangent.at[my_rows, :], cot.at[:, my_cols])]

    barrier = pltpu.get_barrier_semaphore()
    pl.semaphore_signal(barrier, inc=1, device_id=(other, x), device_id_type=MESH)
    for dx in range(1, N_X):
        pl.semaphore_signal(barrier, inc=1, device_id=(me, beyond(dx)), device_id_type=MESH)

    @pl.loop(1, N_CHIP)
    def _(d):
        pl.semaphore_signal(
            barrier, inc=1, device_id=(lax.rem(me + 2 * d, 2 * N_CHIP), x), device_id_type=MESH
        )

    for copy in in_f:
        copy.wait()

    @pl.loop(0, 2)
    def _(t):
        fpart[t] = dot(lens[t], fcols[...]).astype(BF)

    pl.semaphore_wait(barrier, 1 + (N_X - 1) + (N_CHIP - 1))

    sent = []

    def landed(ref, sem):
        pltpu.make_async_copy(ref, ref, sem).wait()

    def remote(src, dst, s, r, device):
        pltpu.make_async_remote_copy(src, dst, s, r, device_id=device, device_id_type=MESH).start()

    def to_other(pairs, whole):
        s, r = sems.new(), sems.new()
        for src, dst in pairs:
            remote(src, dst, s, r, (other, x))
        sent.append((whole, s))
        return lambda: landed(whole, r)

    def to_x(src, dst, whole, which=(1, 3, 2)):
        s, r = sems.new(), sems.new()
        for dx in which:
            remote(src(dx), dst(N_X - dx), s, r, (me, beyond(dx)))
        sent.append((whole, s))
        return lambda: landed(whole, r)

    def to_chips(src, dst, whole):
        s, r = sems.new(), sems.new()

        @pl.loop(1, N_CHIP)
        def _(d):
            peer = lax.rem(chip + d, N_CHIP)
            remote(src(peer), dst(N_CHIP - d), s, r, (2 * peer + core, x))

        sent.append((whole, s))
        return lambda: landed(whole, r)

    def to_line(src, dst, whole, at, step):
        s, r = sems.new(), sems.new()
        for d in (1, 3, 2):
            peer = lax.rem(at + d, N_X)
            remote(src(peer), dst(N_X - d), s, r, (me + 2 * step * (peer - at), x))
        sent.append((whole, s))
        return lambda: landed(whole, r)

    def gather(src, full, fifteen):
        copy = load(src, full)
        done = to_chips(lambda j: src, lambda o: full, fifteen)

        def arrive():
            copy.wait()
            done()

        return arrive

    def add(first, slots, count):
        total = first.astype(F32)
        for o in range(1, count):
            total = total + slots(o).astype(F32)
        return total.astype(BF)

    got_f = to_other([(fpart.at[1 - core], fpair)], fpair)
    got_wo = to_x(lambda dx: w_out.at[piece(chip), mine], lambda o: wo_p.at[o], wo_p.at[1:N_X])
    got_wq = to_x(
        lambda dx: w_query.at[hq, :], lambda o: wqf.at[o, hq, :], wqf.at[0:2, 0:HALF, :], (1, 3)
    )

    @pl.loop(0, 2)
    def _(t):
        @pl.loop(0, 4)
        def _(b):
            at = block(b, 512)
            len_t[t, at, :] = flip(lens[t, :, at])

    got_f()
    fsum[...] = (fpart[core].astype(F32) + fpair[...].astype(F32)).astype(BF)
    got_frs = to_chips(lambda j: fsum.at[piece(j), :], lambda o: frs.at[o], frs.at[1:N_CHIP])
    for copy in in_w:
        copy.wait()
    got_wo()
    got_wof = gather(wo_p, wof.at[:, piece(chip), mine], wof.at[:, 0:240, 0:HALF])
    for copy in in_k + in_q:
        copy.wait()
    got_frs()
    fx[0] = add(fsum[piece(chip), :], lambda o: frs[o], N_CHIP)
    got_fx = to_x(lambda dx: fx.at[0], lambda o: fx.at[o], fx.at[1:N_X])
    q[0] = dot(frows[...], wqf[0]).astype(BF)
    got_fx()
    total = dot(fx[0], wkv[core, my_cols, :])
    for o in range(1, N_X):
        total = total + dot(fx[o], wkv[core, block(beyond(o), WIDTH), :])
    kpx[0] = total.astype(BF)
    got_kpx = to_x(lambda dx: kpx.at[0], lambda o: kpx.at[o], kpx.at[1:N_X])
    got_k = {0: gather(kpx.at[0], kvp.at[core, 0, piece(chip), :], kvp.at[0, 0, 0:240, :])}
    got_wq2 = to_x(lambda dx: w_query.at[hq, :], lambda o: wqf.at[o, hq, :], wqf.at[0, 0:HALF, :], (2,))
    got_cot = to_x(
        lambda dx: cotangent.at[block(beyond(dx), rows), :],
        lambda o: cot.at[:, my_cols],
        cot.at[:, 0 : 3 * WIDTH],
    )
    got_kpx()
    for o in (1, 3, 2):
        got_k[o] = gather(kpx.at[o], kvp.at[core, o, piece(chip), :], kvp.at[0, o, 0:240, :])

    got_wq()
    got_wqo = to_other([(wqf.at[o, hq, :], wqf.at[o, hq, :]) for o in (1, 3)], wqf.at[0:2, 0:HALF, :])
    got_wqo()
    for o in (1, 3):
        q[o] = dot(frows[...], wqf[o]).astype(BF)
    got_kvo = {}

    def pass_on(o):
        got_k[o]()
        got_kvo[o] = to_other([(kvp.at[core, o], kvp.at[core, o])], kvp.at[0, o])

    lane = lax.broadcasted_iota(jnp.int32, (WIDTH, WIDTH), 1) // DH

    def only(h, a):
        return jnp.where(lane == h, a.astype(F32), 0.0).astype(BF)

    def forward(g):
        kg = kvp[0, g]
        vg_t = flip(kvp[1, g])
        qg = q[g]
        for h in range(4):
            scores = dot_nt(only(h, kg), qg)
            top = jnp.max(scores, axis=0, keepdims=True)
            e = jnp.exp((scores - top) * SCALE)
            p = (e * (1.0 / jnp.sum(e, axis=0, keepdims=True))).astype(BF)
            prob[4 * g + h] = p
            att_t[g, h * DH : (h + 1) * DH, :] = dot(vg_t[h * DH : (h + 1) * DH, :], p).astype(BF)
        att[g] = flip(att_t[g])

    pass_on(0)
    got_kvo[0]()
    forward(0)
    pass_on(1)
    got_wq2()
    got_wqo2 = to_other([(wqf.at[2, hq, :], wqf.at[2, hq, :])], wqf.at[0, 0:HALF, :])
    got_wof()
    got_woo = to_other([(wof.at[:, :, mine], wof.at[:, :, mine])], wof.at[:, :, 0:HALF])
    pass_on(3)
    got_kvo[1]()
    forward(1)
    pass_on(2)
    got_ff = gather(fx, ff.at[core, :, piece(chip), :], ff.at[0, :, 0:240, :])
    got_kvo[3]()
    forward(3)
    got_wqo2()
    q[2] = dot(frows[...], wqf[2]).astype(BF)
    got_kvo[2]()
    forward(2)
    got_woo()

    @pl.loop(0, N_X)
    def _(n):
        at = block(beyond(n), WIDTH)
        heads = jnp.concatenate([att[o] for o in range(N_X)], axis=1)
        weights = jnp.concatenate([wof[o, :, at] for o in range(N_X)], axis=0)
        mix_s[n] = dot(heads, weights).astype(BF)

    got_mix = to_x(lambda dx: mix_s.at[dx], lambda o: mix_r.at[my_rows, :], mix_r.at[0 : 3 * rows, :])
    own_mix = load(mix_s.at[0], mix_r.at[my_rows, :])

    for copy in in_c:
        copy.wait()
    got_cot()

    got_wpair, got_wa = ({}, {}), ({}, {})

    def to_pair(k, o):
        got_wpair[k][o] = to_other([(w_s.at[k, o, :, theirs], w_pair.at[k, o])], w_pair.at[k, o])

    def stage_a(k, o):
        got_wpair[k][o]()
        w_sum[k, o] = (w_s[k, o, :, mine].astype(F32) + w_pair[k, o].astype(F32)).astype(BF)
        got_wa[k][o] = to_line(
            lambda p: w_sum.at[k, o, block(p, 64), :], lambda d: w_ra.at[k, o, d], w_ra.at[k, o, 1:N_X], at_a, step_a
        )

    for o in range(N_X):
        w_s[0, o] = dot(att_t[o], cot[...]).astype(BF)
        to_pair(0, o)

    @pl.loop(0, N_X)
    def _(g):
        ga[g] = dot_nt(cot[...], wof[g]).astype(BF)

    for o in range(N_X):
        stage_a(0, o)

    def stage_b(k):
        for o in range(N_X):
            got_wa[k][o]()

        @pl.loop(0, N_X)
        def _(g):
            w_s2[k, g] = add(w_sum[k, g, block(at_a, 64), :], lambda o: w_ra[k, g, o], N_X)

        return to_line(
            lambda p: w_s2.at[k, :, piece(p), :], lambda o: w_rb.at[k, o], w_rb.at[k, 1:N_X], at_b, step_b
        )

    def stage_x(k):
        got_wb[k]()
        w_x[k] = add(w_s2[k, :, piece(at_b), :], lambda o: w_rb[k, o], N_X)
        return to_x(lambda dx: w_x.at[k, dx], lambda o: w_xr.at[k, o], w_xr.at[k, 1:N_X])

    def stage_w(k):
        got_wx[k]()
        w_f[k] = add(w_x[k, 0], lambda o: w_xr[k, o], N_X)
        return gather(w_f.at[k], w_ag.at[k, core, piece(4 * at_a + at_b), :], w_ag.at[k, 0, 0:240, :])

    got_ff()
    got_ffo = to_other([(ff.at[core], ff.at[core])], ff.at[0])

    def backward(g):
        vg = kvp[1, g]
        kg_t = flip(kvp[0, g])
        qg = q[g]
        gag = ga[g]
        gk = jnp.zeros((WIDTH, WIDTH), F32)
        gv = jnp.zeros((WIDTH, WIDTH), F32)
        for h in range(4):
            pb = prob[4 * g + h]
            p = pb.astype(F32)
            gp = dot_nt(only(h, vg), gag)
            inner = jnp.sum(p * gp, axis=0, keepdims=True)
            gs = (p * (gp - inner) * SCALE).astype(BF)
            gq_t[g, h * DH : (h + 1) * DH, :] = dot(kg_t[h * DH : (h + 1) * DH, :], gs).astype(BF)
            gk = jnp.where(lane == h, dot(gs, qg), gk)
            gv = jnp.where(lane == h, dot(pb, gag), gv)
        gkv[0, g] = gk.astype(BF)
        gkv[1, g] = gv.astype(BF)
        gq[g] = flip(gq_t[g])

    order = (1, 2, 3, 0)
    got_gpair, got_grs, got_gx = {}, {}, {}

    def pair_sums(o):
        got_gpair[o]()
        gkv_sum[o] = (gkv[core, o].astype(F32) + gkv_pair[o].astype(F32)).astype(BF)
        got_grs[o] = to_chips(
            lambda j: gkv_sum.at[o, piece(j), :], lambda d: gkv_rs.at[o, d], gkv_rs.at[o, 1:N_CHIP]
        )
        stage_a(1, o)

    def chip_sums(o):
        got_grs[o]()
        gkv_x[o] = add(gkv_sum[o, piece(chip), :], lambda d: gkv_rs[o, d], N_CHIP)
        if o:
            got_gx[o] = to_x(lambda dx: gkv_x.at[dx], lambda d: gkv_xr.at[d], gkv_xr.at[N_X - o], (o,))

    for i, o in enumerate(order):
        backward(o)
        got_gpair[o] = to_other([(gkv.at[1 - core, o], gkv_pair.at[o])], gkv_pair.at[o])
        w_s[1, o] = dot(gq_t[o], frows[...]).astype(BF)
        to_pair(1, o)
        if i > 0:
            pair_sums(order[i - 1])
        if i > 1:
            chip_sums(order[i - 2])
        if i == 2:
            got_wb = [stage_b(0)]
    pair_sums(order[3])
    chip_sums(order[2])
    got_wx = [stage_x(0)]

    @pl.loop(0, N_X)
    def _(n):
        at = block(beyond(n), WIDTH)
        heads = jnp.concatenate([gq[o] for o in range(N_X)], axis=1)
        weights = jnp.concatenate([wqf[o, at, :] for o in range(N_X)], axis=1)
        gf_s[n] = dot_nt(heads, weights).astype(BF)

    def send_gf(which):
        return to_x(
            lambda dx: gf_s.at[dx], lambda o: gf_r.at[my_rows, :], gf_r.at[0 : len(which) * rows, :], which
        )

    got_gf = [send_gf((1, 3))]
    own_gf = load(gf_s.at[0], gf_r.at[my_rows, :])

    chip_sums(0)
    for o in (1, 2, 3):
        got_gx[o]()
    gk16[0] = add(gkv_x[0], lambda o: gkv_xr[o], N_X)
    for o in range(N_X):
        m_s[o] = dot_nt(gk16[0], wkv[core, block(beyond(o), WIDTH), :]).astype(BF)
    got_m = to_x(lambda dx: m_s.at[dx], lambda o: m_r.at[o], m_r.at[1:N_X])
    got_w = [stage_w(0)]
    got_wb.append(stage_b(1))
    got_m()
    gk16[1] = add(m_s[0], lambda o: m_r[o], N_X)
    got_gkm = gather(gk16, gkm.at[core, :, piece(chip), :], gkm.at[0, :, 0:240, :])
    got_wx.append(stage_x(1))
    got_gf.append(send_gf((2,)))
    outs = []
    own_mix.wait()
    got_mix()
    outs.append(load(mix_r, mixed_o))
    got_w[0]()
    got_wo2 = [to_other([(w_ag.at[0, core], w_ag.at[0, core])], w_ag.at[0, 0])]
    got_w.append(stage_w(1))
    got_gkm()
    got_gkmo = to_other([(gkm.at[core], gkm.at[core])], gkm.at[0])
    got_ffo()
    got_gkmo()

    @pl.loop(0, N_X)
    def _(o):
        at = block(beyond(o), WIDTH)
        gwk_v[at, :] = dot(flip(ff[0, o]), gkm[0, 0]).astype(BF)
        gwv_v[at, :] = dot(flip(ff[1, o]), gkm[1, 0]).astype(BF)

    outs.append(load(gwk_v, gwk_o))
    outs.append(load(gwv_v, gwv_o))
    own_gf.wait()
    for wait in got_gf:
        wait()

    @pl.loop(0, N_X)
    def _(b):
        at = block(b, rows)
        total = gf_r[at, :].astype(F32) + dot(len_t[0, at, :], gkm[0, 1]) + dot(len_t[1, at, :], gkm[1, 1])
        gf_r[at, :] = total.astype(BF)

    outs.append(load(gf_r, gframes_o))
    got_wo2[0]()
    outs.append(load(w_ag.at[0], gw_o.at[0]))
    got_w[1]()
    got_wo2.append(to_other([(w_ag.at[1, core], w_ag.at[1, core])], w_ag.at[1, 0]))
    got_wo2[1]()
    outs.append(load(w_ag.at[1], gw_o.at[1]))
    for ref, sem in sent:
        landed(ref, sem)
    for copy in outs:
        copy.wait()


def finish(
    mixed, gframes, gwk, gwv, gw,
    mixed_o, gframes_o, gwq_o, gwk_o, gwv_o, gwo_o,
    raw_k, raw_w, raw_f, wide, wide_o, sem_ref,
):
    sems = Sems(sem_ref)

    def copy(src, dst):
        c = pltpu.make_async_copy(src, dst, sems.new())
        c.start()
        return c

    ins = [copy(gwk, raw_k.at[0]), copy(gwv, raw_k.at[1]), copy(gw.at[0], raw_w.at[0]), copy(gw.at[1], raw_w.at[1])]
    through = [copy(mixed, raw_f.at[0]), copy(gframes, raw_f.at[1])]
    outs = []
    for k, out in enumerate((gwk_o, gwv_o)):
        ins[k].wait()
        wide[k] = raw_k[k].astype(F32)
        outs.append(copy(wide.at[k], out))
    for k, out in enumerate((mixed_o, gframes_o)):
        through[k].wait()
        outs.append(copy(raw_f.at[k], out))
    ins[2].wait()
    for t in range(2):
        wide_o[:, t * HALF : (t + 1) * HALF] = raw_w[0, t].astype(F32)
    outs.append(copy(wide_o, gwo_o))
    ins[3].wait()
    for t in range(2):
        wide[2, t * HALF : (t + 1) * HALF, :] = raw_w[1, t].astype(F32).T
    outs.append(copy(wide.at[2], gwq_o))
    for c in outs:
        c.wait()


def body(frames, len_keys, len_values, w_query, w_key, w_value, w_out, cotangent):
    span, depth = frames.shape
    rows = span // N_X

    def bf(*shape):
        return pltpu.VMEM(shape, BF)

    scratch = [
        bf(span, 256), bf(rows, depth), bf(2, 256, span), bf(2, span, 256),
        bf(4, 1024, 256), bf(4, 256, 1024), bf(4, 16, 512), bf(2, 1024, 256), bf(rows, depth),
        bf(2, 256, 256), bf(256, 256), bf(256, 256), bf(16, 16, 256),
        bf(4, 16, 256), bf(4, 16, 256), bf(2, 4, 256, 256), bf(2, 4, 256, 256),
        bf(4, rows, 256), bf(4, rows, 256), bf(16, 256, rows),
        bf(4, 256, rows), bf(4, rows, 256), bf(4, 256, rows), bf(4, rows, 256),
        bf(4, rows, 256), bf(span, 256), bf(4, rows, 256), bf(span, 256),
        bf(2, 4, 256, 256), bf(4, 256, 256), bf(4, 256, 256), bf(4, 16, 16, 256),
        bf(4, 16, 256), bf(4, 16, 256), bf(2, 16, 256), bf(4, 16, 256), bf(4, 16, 256),
        bf(2, 2, 256, 256),
        bf(2, 4, 256, 1024), bf(2, 4, 256, 512), bf(2, 4, 256, 512), bf(2, 4, 4, 64, 512),
        bf(2, 4, 64, 512), bf(2, 4, 4, 16, 512), bf(2, 4, 16, 512), bf(2, 4, 16, 512),
        bf(2, 16, 512), bf(2, 2, 256, 512), bf(depth, 256), bf(depth, 256),
        pltpu.SemaphoreType.DMA((180,)),
    ]
    any_ = pl.BlockSpec(memory_space=pl.ANY)
    shape = jax.ShapeDtypeStruct
    raw = pl.pallas_call(
        kernel,
        out_shape=(
            shape((span, 256), BF), shape((span, 256), BF),
            shape((depth, 256), BF), shape((depth, 256), BF), shape((2, 2, 256, 512), BF),
        ),
        in_specs=[any_] * 8,
        out_specs=(any_,) * 5,
        scratch_shapes=scratch,
        compiler_params=pltpu.CompilerParams(
            collective_id=0, has_side_effects=True, vmem_limit_bytes=60 * 1024 * 1024
        ),
        cost_estimate=pl.CostEstimate(flops=14_000_000_000, bytes_accessed=24_000_000, transcendentals=2_097_152),
    )(frames, len_keys, len_values, w_query, w_key, w_value, w_out, cotangent)
    return pl.pallas_call(
        finish,
        out_shape=(
            shape((span, 256), BF), shape((span, 256), BF),
            shape((depth, 256), F32), shape((depth, 256), F32), shape((depth, 256), F32), shape((256, depth), F32),
        ),
        in_specs=[any_] * 5,
        out_specs=(any_,) * 6,
        scratch_shapes=[
            bf(2, depth, 256), bf(2, 2, 256, 512), bf(2, span, 256),
            pltpu.VMEM((3, depth, 256), F32), pltpu.VMEM((256, depth), F32),
            pltpu.SemaphoreType.DMA((12,)),
        ],
        compiler_params=pltpu.CompilerParams(vmem_limit_bytes=60 * 1024 * 1024),
        cost_estimate=pl.CostEstimate(flops=1_000_000, bytes_accessed=11_000_000, transcendentals=0),
    )(*raw)


def solution(mesh):
    placed = (
        P("ctx", None),
        P(None, "ctx"),
        P(None, "ctx"),
        P(None, "head"),
        P(None, "head"),
        P(None, "head"),
        P("head", None),
        P("ctx", "head"),
    )
    return jax.shard_map(
        body,
        mesh=mesh,
        in_specs=placed,
        out_specs=(
            P("ctx", "head"),
            P("ctx", "head"),
            P(None, "head"),
            P(None, "head"),
            P(None, "head"),
            P("head", None),
        ),
        check_vma=False,
    )
```

```python
import jax
import jax.numpy as jnp
from jax import lax
from jax.experimental import pallas as pl
from jax.experimental.pallas import tpu as pltpu
from jax.sharding import PartitionSpec as P

DH = 64
SCALE = DH ** -0.5
N_X = 4
N_CHIP = 16
WIDTH = 256
HALF = 512
MESH = pl.DeviceIdType.MESH
BF = jnp.bfloat16
F32 = jnp.float32


def dot(a, b):
    return jnp.dot(a, b, preferred_element_type=F32)


def dot_nt(a, b):
    return lax.dot_general(a, b, (((1,), (1,)), ((), ())), preferred_element_type=F32)


def flip(a):
    return a.astype(F32).T.astype(BF)


class Sems:
    def __init__(self, ref):
        self.ref, self.used = ref, 0

    def new(self):
        self.used += 1
        return self.ref.at[self.used - 1]


def kernel(
    frames, len_keys, len_values, w_query, w_key, w_value, w_out, cotangent,
    mixed_o, gframes_o, gwk_o, gwv_o, gw_o,
    fcols, frows, lens, len_t, wqf, wof, wo_p, wkv, cot,
    fpart, fpair, fsum, frs, fx, kpx, ff, kvp,
    q, ga, prob, att_t, att, gq_t, gq,
    mix_s, mix_r, gf_s, gf_r,
    gkv, gkv_pair, gkv_sum, gkv_rs, gkv_x, gkv_xr, gk16, m_s, m_r, gkm,
    w_s, w_pair, w_sum, w_ra, w_s2, w_rb, w_x, w_xr, w_f, w_ag, gwk_v, gwv_v, sem_ref,
):
    sems = Sems(sem_ref)
    me = lax.axis_index("ctx")
    x = lax.axis_index("head")
    core = lax.rem(me, 2)
    chip = lax.div(me, 2)
    other = me + 1 - 2 * core
    rows = frows.shape[0]
    step_a = 1 + 3 * core
    step_b = 4 - 3 * core
    at_a = lax.rem(lax.div(chip, step_a), N_X)
    at_b = lax.rem(lax.div(chip, step_b), N_X)

    def block(i, size):
        return pl.ds(pl.multiple_of(i * size, size), size)

    def beyond(o):
        return lax.rem(x + o, N_X)

    def piece(i):
        return block(i, 16)

    my_cols = block(x, WIDTH)
    my_rows = block(x, rows)
    mine = block(core, HALF)
    theirs = block(1 - core, HALF)
    hq = block(core, HALF)

    def load(src, dst):
        copy = pltpu.make_async_copy(src, dst, sems.new())
        copy.start()
        return copy

    in_f = [load(frames.at[:, my_cols], fcols), load(len_keys, lens.at[0]), load(len_values, lens.at[1])]
    in_w = [load(w_out, wof.at[0])]
    in_k = [load(w_key, wkv.at[0]), load(w_value, wkv.at[1])]
    in_q = [load(frames.at[my_rows, :], frows), load(w_query, wqf.at[0])]
    in_c = [load(cotangent.at[my_rows, :], cot.at[:, my_cols])]

    barrier = pltpu.get_barrier_semaphore()
    pl.semaphore_signal(barrier, inc=1, device_id=(other, x), device_id_type=MESH)
    for dx in range(1, N_X):
        pl.semaphore_signal(barrier, inc=1, device_id=(me, beyond(dx)), device_id_type=MESH)

    @pl.loop(1, N_CHIP)
    def _(d):
        pl.semaphore_signal(
            barrier, inc=1, device_id=(lax.rem(me + 2 * d, 2 * N_CHIP), x), device_id_type=MESH
        )

    for copy in in_f:
        copy.wait()

    @pl.loop(0, 2)
    def _(t):
        fpart[t] = dot(lens[t], fcols[...]).astype(BF)

    pl.semaphore_wait(barrier, 1 + (N_X - 1) + (N_CHIP - 1))

    sent = []

    def landed(ref, sem):
        pltpu.make_async_copy(ref, ref, sem).wait()

    def remote(src, dst, s, r, device):
        pltpu.make_async_remote_copy(src, dst, s, r, device_id=device, device_id_type=MESH).start()

    def to_other(pairs, whole):
        s, r = sems.new(), sems.new()
        for src, dst in pairs:
            remote(src, dst, s, r, (other, x))
        sent.append((whole, s))
        return lambda: landed(whole, r)

    def to_x(src, dst, whole, which=(1, 3, 2)):
        s, r = sems.new(), sems.new()
        for dx in which:
            remote(src(dx), dst(N_X - dx), s, r, (me, beyond(dx)))
        sent.append((whole, s))
        return lambda: landed(whole, r)

    def to_chips(src, dst, whole):
        s, r = sems.new(), sems.new()

        @pl.loop(1, N_CHIP)
        def _(d):
            peer = lax.rem(chip + d, N_CHIP)
            remote(src(peer), dst(N_CHIP - d), s, r, (2 * peer + core, x))

        sent.append((whole, s))
        return lambda: landed(whole, r)

    def to_line(src, dst, whole, at, step):
        s, r = sems.new(), sems.new()
        for d in (1, 3, 2):
            peer = lax.rem(at + d, N_X)
            remote(src(peer), dst(N_X - d), s, r, (me + 2 * step * (peer - at), x))
        sent.append((whole, s))
        return lambda: landed(whole, r)

    def gather(src, full, fifteen):
        copy = load(src, full)
        done = to_chips(lambda j: src, lambda o: full, fifteen)

        def arrive():
            copy.wait()
            done()

        return arrive

    def add(first, slots, count):
        total = first.astype(F32)
        for o in range(1, count):
            total = total + slots(o).astype(F32)
        return total.astype(BF)

    got_f = to_other([(fpart.at[1 - core], fpair)], fpair)
    got_wo = to_x(lambda dx: w_out.at[piece(chip), mine], lambda o: wo_p.at[o], wo_p.at[1:N_X])
    got_wq = to_x(
        lambda dx: w_query.at[hq, :], lambda o: wqf.at[o, hq, :], wqf.at[0:2, 0:HALF, :], (1, 3)
    )

    @pl.loop(0, 2)
    def _(t):
        @pl.loop(0, 4)
        def _(b):
            at = block(b, 512)
            len_t[t, at, :] = flip(lens[t, :, at])

    got_f()
    fsum[...] = (fpart[core].astype(F32) + fpair[...].astype(F32)).astype(BF)
    got_frs = to_chips(lambda j: fsum.at[piece(j), :], lambda o: frs.at[o], frs.at[1:N_CHIP])
    got_wo()
    got_wof = gather(
        wo_p.at[1:N_X], wof.at[1:N_X, piece(chip), mine], wof.at[1:N_X, 0:240, 0:HALF]
    )
    for copy in in_w:
        copy.wait()
    for copy in in_k + in_q:
        copy.wait()
    got_frs()
    fx[0] = add(fsum[piece(chip), :], lambda o: frs[o], N_CHIP)
    got_fx = to_x(lambda dx: fx.at[0], lambda o: fx.at[o], fx.at[1:N_X])
    q[0] = dot(frows[...], wqf[0]).astype(BF)
    got_fx()
    total = dot(fx[0], wkv[core, my_cols, :])
    for o in range(1, N_X):
        total = total + dot(fx[o], wkv[core, block(beyond(o), WIDTH), :])
    kpx[0] = total.astype(BF)
    got_kpx = to_x(lambda dx: kpx.at[0], lambda o: kpx.at[o], kpx.at[1:N_X])
    got_k = {0: gather(kpx.at[0], kvp.at[core, 0, piece(chip), :], kvp.at[0, 0, 0:240, :])}
    got_wq2 = to_x(lambda dx: w_query.at[hq, :], lambda o: wqf.at[o, hq, :], wqf.at[0, 0:HALF, :], (2,))
    got_cot = to_x(
        lambda dx: cotangent.at[block(beyond(dx), rows), :],
        lambda o: cot.at[:, my_cols],
        cot.at[:, 0 : 3 * WIDTH],
    )
    got_kpx()
    for o in (1, 3, 2):
        got_k[o] = gather(kpx.at[o], kvp.at[core, o, piece(chip), :], kvp.at[0, o, 0:240, :])

    got_wq()
    got_wqo = to_other([(wqf.at[o, hq, :], wqf.at[o, hq, :]) for o in (1, 3)], wqf.at[0:2, 0:HALF, :])
    got_wqo()
    for o in (1, 3):
        q[o] = dot(frows[...], wqf[o]).astype(BF)
    got_kvo = {}

    def pass_on(o):
        got_k[o]()
        got_kvo[o] = to_other([(kvp.at[core, o], kvp.at[core, o])], kvp.at[0, o])

    lane = lax.broadcasted_iota(jnp.int32, (WIDTH, WIDTH), 1) // DH

    def only(h, a):
        return jnp.where(lane == h, a.astype(F32), 0.0).astype(BF)

    def forward(g):
        kg = kvp[0, g]
        vg_t = flip(kvp[1, g])
        qg = q[g]
        for h in range(4):
            scores = dot_nt(only(h, kg), qg)
            top = jnp.max(scores, axis=0, keepdims=True)
            e = jnp.exp((scores - top) * SCALE)
            p = (e * (1.0 / jnp.sum(e, axis=0, keepdims=True))).astype(BF)
            prob[4 * g + h] = p
            att_t[g, h * DH : (h + 1) * DH, :] = dot(vg_t[h * DH : (h + 1) * DH, :], p).astype(BF)
        att[g] = flip(att_t[g])

    pass_on(0)
    got_kvo[0]()
    forward(0)
    pass_on(1)
    got_wq2()
    got_wqo2 = to_other([(wqf.at[2, hq, :], wqf.at[2, hq, :])], wqf.at[0, 0:HALF, :])
    got_wof()
    got_woo = to_other([(wof.at[1:N_X, :, mine], wof.at[1:N_X, :, mine])], wof.at[1:N_X, :, 0:HALF])
    pass_on(3)
    got_kvo[1]()
    forward(1)
    pass_on(2)
    got_ff = gather(fx, ff.at[core, :, piece(chip), :], ff.at[0, :, 0:240, :])
    got_kvo[3]()
    forward(3)
    got_wqo2()
    q[2] = dot(frows[...], wqf[2]).astype(BF)
    got_kvo[2]()
    forward(2)

    def mix():
        @pl.loop(0, N_X)
        def _(n):
            at = block(beyond(n), WIDTH)
            heads = jnp.concatenate([att[o] for o in range(N_X)], axis=1)
            weights = jnp.concatenate([wof[o, :, at] for o in range(N_X)], axis=0)
            mix_s[n] = dot(heads, weights).astype(BF)

        arrived = to_x(lambda dx: mix_s.at[dx], lambda o: mix_r.at[my_rows, :], mix_r.at[0 : 3 * rows, :])
        return arrived, load(mix_s.at[0], mix_r.at[my_rows, :])

    for copy in in_c:
        copy.wait()
    got_cot()

    got_wpair, got_wa = ({}, {}), ({}, {})

    def to_pair(k, o):
        got_wpair[k][o] = to_other([(w_s.at[k, o, :, theirs], w_pair.at[k, o])], w_pair.at[k, o])

    def stage_a(k, o):
        got_wpair[k][o]()
        w_sum[k, o] = (w_s[k, o, :, mine].astype(F32) + w_pair[k, o].astype(F32)).astype(BF)
        got_wa[k][o] = to_line(
            lambda p: w_sum.at[k, o, block(p, 64), :], lambda d: w_ra.at[k, o, d], w_ra.at[k, o, 1:N_X], at_a, step_a
        )

    for o in range(N_X):
        w_s[0, o] = dot(att_t[o], cot[...]).astype(BF)
        to_pair(0, o)

    got_woo()

    @pl.loop(0, N_X)
    def _(g):
        ga[g] = dot_nt(cot[...], wof[g]).astype(BF)

    for o in range(N_X):
        stage_a(0, o)

    def stage_b(k):
        for o in range(N_X):
            got_wa[k][o]()

        @pl.loop(0, N_X)
        def _(g):
            w_s2[k, g] = add(w_sum[k, g, block(at_a, 64), :], lambda o: w_ra[k, g, o], N_X)

        return to_line(
            lambda p: w_s2.at[k, :, piece(p), :], lambda o: w_rb.at[k, o], w_rb.at[k, 1:N_X], at_b, step_b
        )

    def stage_x(k):
        got_wb[k]()
        w_x[k] = add(w_s2[k, :, piece(at_b), :], lambda o: w_rb[k, o], N_X)
        return to_x(lambda dx: w_x.at[k, dx], lambda o: w_xr.at[k, o], w_xr.at[k, 1:N_X])

    def stage_w(k):
        got_wx[k]()
        w_f[k] = add(w_x[k, 0], lambda o: w_xr[k, o], N_X)
        return gather(w_f.at[k], w_ag.at[k, core, piece(4 * at_a + at_b), :], w_ag.at[k, 0, 0:240, :])

    got_ff()
    got_ffo = to_other([(ff.at[core], ff.at[core])], ff.at[0])

    def backward(g):
        vg = kvp[1, g]
        kg_t = flip(kvp[0, g])
        qg = q[g]
        gag = ga[g]
        gk = jnp.zeros((WIDTH, WIDTH), F32)
        gv = jnp.zeros((WIDTH, WIDTH), F32)
        for h in range(4):
            pb = prob[4 * g + h]
            p = pb.astype(F32)
            gp = dot_nt(only(h, vg), gag)
            inner = jnp.sum(p * gp, axis=0, keepdims=True)
            gs = (p * (gp - inner) * SCALE).astype(BF)
            gq_t[g, h * DH : (h + 1) * DH, :] = dot(kg_t[h * DH : (h + 1) * DH, :], gs).astype(BF)
            gk = jnp.where(lane == h, dot(gs, qg), gk)
            gv = jnp.where(lane == h, dot(pb, gag), gv)
        gkv[0, g] = gk.astype(BF)
        gkv[1, g] = gv.astype(BF)
        gq[g] = flip(gq_t[g])

    order = (1, 2, 3, 0)
    got_gpair, got_grs, got_gx = {}, {}, {}

    def pair_sums(o):
        got_gpair[o]()
        gkv_sum[o] = (gkv[core, o].astype(F32) + gkv_pair[o].astype(F32)).astype(BF)
        got_grs[o] = to_chips(
            lambda j: gkv_sum.at[o, piece(j), :], lambda d: gkv_rs.at[o, d], gkv_rs.at[o, 1:N_CHIP]
        )
        stage_a(1, o)

    def chip_sums(o):
        got_grs[o]()
        gkv_x[o] = add(gkv_sum[o, piece(chip), :], lambda d: gkv_rs[o, d], N_CHIP)
        if o:
            got_gx[o] = to_x(lambda dx: gkv_x.at[dx], lambda d: gkv_xr.at[d], gkv_xr.at[N_X - o], (o,))

    for i, o in enumerate(order):
        backward(o)
        got_gpair[o] = to_other([(gkv.at[1 - core, o], gkv_pair.at[o])], gkv_pair.at[o])
        w_s[1, o] = dot(gq_t[o], frows[...]).astype(BF)
        to_pair(1, o)
        if i == 0:
            got_mix, own_mix = mix()
        if i > 0:
            pair_sums(order[i - 1])
        if i > 1:
            chip_sums(order[i - 2])
        if i == 2:
            got_wb = [stage_b(0)]
    pair_sums(order[3])
    chip_sums(order[2])
    got_wx = [stage_x(0)]

    @pl.loop(0, N_X)
    def _(n):
        at = block(beyond(n), WIDTH)
        heads = jnp.concatenate([gq[o] for o in range(N_X)], axis=1)
        weights = jnp.concatenate([wqf[o, at, :] for o in range(N_X)], axis=1)
        gf_s[n] = dot_nt(heads, weights).astype(BF)

    def send_gf(which):
        return to_x(
            lambda dx: gf_s.at[dx], lambda o: gf_r.at[my_rows, :], gf_r.at[0 : len(which) * rows, :], which
        )

    got_gf = [send_gf((1, 3))]
    own_gf = load(gf_s.at[0], gf_r.at[my_rows, :])

    chip_sums(0)
    for o in (1, 2, 3):
        got_gx[o]()
    gk16[0] = add(gkv_x[0], lambda o: gkv_xr[o], N_X)
    for o in range(N_X):
        m_s[o] = dot_nt(gk16[0], wkv[core, block(beyond(o), WIDTH), :]).astype(BF)
    got_m = to_x(lambda dx: m_s.at[dx], lambda o: m_r.at[o], m_r.at[1:N_X])
    got_w = [stage_w(0)]
    got_wb.append(stage_b(1))
    got_m()
    gk16[1] = add(m_s[0], lambda o: m_r[o], N_X)
    got_gkm = gather(gk16, gkm.at[core, :, piece(chip), :], gkm.at[0, :, 0:240, :])
    got_wx.append(stage_x(1))
    got_gf.append(send_gf((2,)))
    outs = []
    got_w.append(stage_w(1))
    got_gkm()
    got_gkmo = to_other([(gkm.at[core], gkm.at[core])], gkm.at[0])
    got_w[0]()
    got_wo2 = [to_other([(w_ag.at[0, core], w_ag.at[0, core])], w_ag.at[0, 0])]
    own_mix.wait()
    got_mix()
    outs.append(load(mix_r, mixed_o))
    got_ffo()
    got_gkmo()

    @pl.loop(0, N_X)
    def _(o):
        at = block(beyond(o), WIDTH)
        gwk_v[at, :] = dot(flip(ff[0, o]), gkm[0, 0]).astype(BF)
        gwv_v[at, :] = dot(flip(ff[1, o]), gkm[1, 0]).astype(BF)

    outs.append(load(gwk_v, gwk_o))
    outs.append(load(gwv_v, gwv_o))
    own_gf.wait()
    for wait in got_gf:
        wait()

    @pl.loop(0, N_X)
    def _(b):
        at = block(b, rows)
        total = gf_r[at, :].astype(F32) + dot(len_t[0, at, :], gkm[0, 1]) + dot(len_t[1, at, :], gkm[1, 1])
        gf_r[at, :] = total.astype(BF)

    outs.append(load(gf_r, gframes_o))
    got_wo2[0]()
    outs.append(load(w_ag.at[0], gw_o.at[0]))
    got_w[1]()
    got_wo2.append(to_other([(w_ag.at[1, core], w_ag.at[1, core])], w_ag.at[1, 0]))
    got_wo2[1]()
    outs.append(load(w_ag.at[1], gw_o.at[1]))
    for ref, sem in sent:
        landed(ref, sem)
    for copy in outs:
        copy.wait()


def finish(
    mixed, gframes, gwk, gwv, gw,
    mixed_o, gframes_o, gwq_o, gwk_o, gwv_o, gwo_o,
    raw_k, raw_w, raw_f, wide, wide_o, sem_ref,
):
    sems = Sems(sem_ref)

    def copy(src, dst):
        c = pltpu.make_async_copy(src, dst, sems.new())
        c.start()
        return c

    ins = [copy(gwk, raw_k.at[0]), copy(gwv, raw_k.at[1]), copy(gw.at[0], raw_w.at[0]), copy(gw.at[1], raw_w.at[1])]
    through = [copy(mixed, raw_f.at[0]), copy(gframes, raw_f.at[1])]
    outs = []
    for k, out in enumerate((gwk_o, gwv_o)):
        ins[k].wait()
        wide[k] = raw_k[k].astype(F32)
        outs.append(copy(wide.at[k], out))
    for k, out in enumerate((mixed_o, gframes_o)):
        through[k].wait()
        outs.append(copy(raw_f.at[k], out))
    ins[2].wait()
    for t in range(2):
        wide_o[:, t * HALF : (t + 1) * HALF] = raw_w[0, t].astype(F32)
    outs.append(copy(wide_o, gwo_o))
    ins[3].wait()
    for t in range(2):
        wide[2, t * HALF : (t + 1) * HALF, :] = raw_w[1, t].astype(F32).T
    outs.append(copy(wide.at[2], gwq_o))
    for c in outs:
        c.wait()


def body(frames, len_keys, len_values, w_query, w_key, w_value, w_out, cotangent):
    span, depth = frames.shape
    rows = span // N_X

    def bf(*shape):
        return pltpu.VMEM(shape, BF)

    scratch = [
        bf(span, 256), bf(rows, depth), bf(2, 256, span), bf(2, span, 256),
        bf(4, 1024, 256), bf(4, 256, 1024), bf(4, 16, 512), bf(2, 1024, 256), bf(rows, depth),
        bf(2, 256, 256), bf(256, 256), bf(256, 256), bf(16, 16, 256),
        bf(4, 16, 256), bf(4, 16, 256), bf(2, 4, 256, 256), bf(2, 4, 256, 256),
        bf(4, rows, 256), bf(4, rows, 256), bf(16, 256, rows),
        bf(4, 256, rows), bf(4, rows, 256), bf(4, 256, rows), bf(4, rows, 256),
        bf(4, rows, 256), bf(span, 256), bf(4, rows, 256), bf(span, 256),
        bf(2, 4, 256, 256), bf(4, 256, 256), bf(4, 256, 256), bf(4, 16, 16, 256),
        bf(4, 16, 256), bf(4, 16, 256), bf(2, 16, 256), bf(4, 16, 256), bf(4, 16, 256),
        bf(2, 2, 256, 256),
        bf(2, 4, 256, 1024), bf(2, 4, 256, 512), bf(2, 4, 256, 512), bf(2, 4, 4, 64, 512),
        bf(2, 4, 64, 512), bf(2, 4, 4, 16, 512), bf(2, 4, 16, 512), bf(2, 4, 16, 512),
        bf(2, 16, 512), bf(2, 2, 256, 512), bf(depth, 256), bf(depth, 256),
        pltpu.SemaphoreType.DMA((180,)),
    ]
    any_ = pl.BlockSpec(memory_space=pl.ANY)
    shape = jax.ShapeDtypeStruct
    raw = pl.pallas_call(
        kernel,
        out_shape=(
            shape((span, 256), BF), shape((span, 256), BF),
            shape((depth, 256), BF), shape((depth, 256), BF), shape((2, 2, 256, 512), BF),
        ),
        in_specs=[any_] * 8,
        out_specs=(any_,) * 5,
        scratch_shapes=scratch,
        compiler_params=pltpu.CompilerParams(
            collective_id=0, has_side_effects=True, vmem_limit_bytes=60 * 1024 * 1024
        ),
        cost_estimate=pl.CostEstimate(flops=14_000_000_000, bytes_accessed=24_000_000, transcendentals=2_097_152),
    )(frames, len_keys, len_values, w_query, w_key, w_value, w_out, cotangent)
    return pl.pallas_call(
        finish,
        out_shape=(
            shape((span, 256), BF), shape((span, 256), BF),
            shape((depth, 256), F32), shape((depth, 256), F32), shape((depth, 256), F32), shape((256, depth), F32),
        ),
        in_specs=[any_] * 5,
        out_specs=(any_,) * 6,
        scratch_shapes=[
            bf(2, depth, 256), bf(2, 2, 256, 512), bf(2, span, 256),
            pltpu.VMEM((3, depth, 256), F32), pltpu.VMEM((256, depth), F32),
            pltpu.SemaphoreType.DMA((12,)),
        ],
        compiler_params=pltpu.CompilerParams(vmem_limit_bytes=60 * 1024 * 1024),
        cost_estimate=pl.CostEstimate(flops=1_000_000, bytes_accessed=11_000_000, transcendentals=0),
    )(*raw)


def solution(mesh):
    placed = (
        P("ctx", None),
        P(None, "ctx"),
        P(None, "ctx"),
        P(None, "head"),
        P(None, "head"),
        P(None, "head"),
        P("head", None),
        P("ctx", "head"),
    )
    return jax.shard_map(
        body,
        mesh=mesh,
        in_specs=placed,
        out_specs=(
            P("ctx", "head"),
            P("ctx", "head"),
            P(None, "head"),
            P(None, "head"),
            P(None, "head"),
            P("head", None),
        ),
        check_vma=False,
    )
```

```python
import jax
import jax.numpy as jnp
from jax import lax
from jax.experimental import pallas as pl
from jax.experimental.pallas import tpu as pltpu
from jax.sharding import PartitionSpec as P

DH = 64
SCALE = DH ** -0.5
N_X = 4
N_CHIP = 16
WIDTH = 256
HALF = 512
MESH = pl.DeviceIdType.MESH
BF = jnp.bfloat16
F32 = jnp.float32


def dot(a, b):
    return jnp.dot(a, b, preferred_element_type=F32)


def dot_nt(a, b):
    return lax.dot_general(a, b, (((1,), (1,)), ((), ())), preferred_element_type=F32)


def flip(a):
    return a.astype(F32).T.astype(BF)


class Sems:
    def __init__(self, ref):
        self.ref, self.used = ref, 0

    def new(self):
        self.used += 1
        return self.ref.at[self.used - 1]


def kernel(
    frames, len_keys, len_values, w_query, w_key, w_value, w_out, cotangent,
    mixed_o, gframes_o, gwk_o, gwv_o, gw_o,
    fcols, frows, lens, len_t, wqf, wof, wo_p, wkv, cot,
    fpart, fpair, fsum, frs, fx, kpx, ff, kvp,
    q, ga, prob, att_t, att, gq_t, gq,
    mix_s, mix_r, gf_s, gf_r,
    gkv, gkv_pair, gkv_sum, gkv_rs, gkv_x, gkv_xr, gk16, m_s, m_r, gkm,
    w_s, w_pair, w_sum, w_ra, w_s2, w_rb, w_x, w_xr, w_f, w_ag, gwk_v, gwv_v, sem_ref,
):
    sems = Sems(sem_ref)
    me = lax.axis_index("ctx")
    x = lax.axis_index("head")
    core = lax.rem(me, 2)
    chip = lax.div(me, 2)
    other = me + 1 - 2 * core
    rows = frows.shape[0]
    step_a = 1 + 3 * core
    step_b = 4 - 3 * core
    at_a = lax.rem(lax.div(chip, step_a), N_X)
    at_b = lax.rem(lax.div(chip, step_b), N_X)

    def block(i, size):
        return pl.ds(pl.multiple_of(i * size, size), size)

    def beyond(o):
        return lax.rem(x + o, N_X)

    def piece(i):
        return block(i, 16)

    my_cols = block(x, WIDTH)
    my_rows = block(x, rows)
    mine = block(core, HALF)
    theirs = block(1 - core, HALF)
    hq = block(core, HALF)

    def load(src, dst):
        copy = pltpu.make_async_copy(src, dst, sems.new())
        copy.start()
        return copy

    in_f = [load(frames.at[:, my_cols], fcols), load(len_keys, lens.at[0]), load(len_values, lens.at[1])]
    in_w = [load(w_out, wof.at[0])]
    in_k = [load(w_key, wkv.at[0]), load(w_value, wkv.at[1])]
    in_q = [load(frames.at[my_rows, :], frows), load(w_query, wqf.at[0])]
    in_c = [load(cotangent.at[my_rows, :], cot.at[:, my_cols])]

    barrier = pltpu.get_barrier_semaphore()
    pl.semaphore_signal(barrier, inc=1, device_id=(other, x), device_id_type=MESH)
    for dx in range(1, N_X):
        pl.semaphore_signal(barrier, inc=1, device_id=(me, beyond(dx)), device_id_type=MESH)

    @pl.loop(1, N_CHIP)
    def _(d):
        pl.semaphore_signal(
            barrier, inc=1, device_id=(lax.rem(me + 2 * d, 2 * N_CHIP), x), device_id_type=MESH
        )

    for copy in in_f:
        copy.wait()

    @pl.loop(0, 2)
    def _(t):
        fpart[t] = dot(lens[t], fcols[...]).astype(BF)

    pl.semaphore_wait(barrier, 1 + (N_X - 1) + (N_CHIP - 1))

    sent = []

    def landed(ref, sem):
        pltpu.make_async_copy(ref, ref, sem).wait()

    def remote(src, dst, s, r, device):
        pltpu.make_async_remote_copy(src, dst, s, r, device_id=device, device_id_type=MESH).start()

    def to_other(pairs, whole):
        s, r = sems.new(), sems.new()
        for src, dst in pairs:
            remote(src, dst, s, r, (other, x))
        sent.append((whole, s))
        return lambda: landed(whole, r)

    def to_x(src, dst, whole, which=(1, 3, 2)):
        s, r = sems.new(), sems.new()
        for dx in which:
            remote(src(dx), dst(N_X - dx), s, r, (me, beyond(dx)))
        sent.append((whole, s))
        return lambda: landed(whole, r)

    def to_chips(src, dst, whole):
        s, r = sems.new(), sems.new()

        @pl.loop(1, N_CHIP)
        def _(d):
            peer = lax.rem(chip + d, N_CHIP)
            remote(src(peer), dst(N_CHIP - d), s, r, (2 * peer + core, x))

        sent.append((whole, s))
        return lambda: landed(whole, r)

    def to_line(src, dst, whole, at, step):
        s, r = sems.new(), sems.new()
        for d in (1, 3, 2):
            peer = lax.rem(at + d, N_X)
            remote(src(peer), dst(N_X - d), s, r, (me + 2 * step * (peer - at), x))
        sent.append((whole, s))
        return lambda: landed(whole, r)

    def gather(src, full, fifteen):
        copy = load(src, full)
        done = to_chips(lambda j: src, lambda o: full, fifteen)

        def arrive():
            copy.wait()
            done()

        return arrive

    def add(first, slots, count):
        total = first.astype(F32)
        for o in range(1, count):
            total = total + slots(o).astype(F32)
        return total.astype(BF)

    got_f = to_other([(fpart.at[1 - core], fpair)], fpair)
    got_wo = to_x(lambda dx: w_out.at[piece(chip), mine], lambda o: wo_p.at[o], wo_p.at[1:N_X])
    got_wq = to_x(
        lambda dx: w_query.at[hq, :], lambda o: wqf.at[o, hq, :], wqf.at[0:2, 0:HALF, :], (1, 3)
    )

    @pl.loop(0, 2)
    def _(t):
        @pl.loop(0, 4)
        def _(b):
            at = block(b, 512)
            len_t[t, at, :] = flip(lens[t, :, at])

    got_f()
    fsum[...] = (fpart[core].astype(F32) + fpair[...].astype(F32)).astype(BF)
    got_frs = to_chips(lambda j: fsum.at[piece(j), :], lambda o: frs.at[o], frs.at[1:N_CHIP])
    got_wo()
    got_wof = gather(
        wo_p.at[1:N_X], wof.at[1:N_X, piece(chip), mine], wof.at[1:N_X, 0:240, 0:HALF]
    )
    for copy in in_w:
        copy.wait()
    for copy in in_k + in_q:
        copy.wait()
    got_frs()
    fx[0] = add(fsum[piece(chip), :], lambda o: frs[o], N_CHIP)
    got_fx = to_x(lambda dx: fx.at[0], lambda o: fx.at[o], fx.at[1:N_X])
    q[0] = dot(frows[...], wqf[0]).astype(BF)
    got_fx()
    total = dot(fx[0], wkv[core, my_cols, :])
    for o in range(1, N_X):
        total = total + dot(fx[o], wkv[core, block(beyond(o), WIDTH), :])
    kpx[0] = total.astype(BF)
    got_kpx = to_x(lambda dx: kpx.at[0], lambda o: kpx.at[o], kpx.at[1:N_X])
    got_k = {0: gather(kpx.at[0], kvp.at[core, 0, piece(chip), :], kvp.at[0, 0, 0:240, :])}
    got_wq2 = to_x(lambda dx: w_query.at[hq, :], lambda o: wqf.at[o, hq, :], wqf.at[0, 0:HALF, :], (2,))
    got_cot = to_x(
        lambda dx: cotangent.at[block(beyond(dx), rows), :],
        lambda o: cot.at[:, my_cols],
        cot.at[:, 0 : 3 * WIDTH],
    )
    got_kpx()
    for o in (1, 3, 2):
        got_k[o] = gather(kpx.at[o], kvp.at[core, o, piece(chip), :], kvp.at[0, o, 0:240, :])

    got_wq()
    got_wqo = to_other([(wqf.at[o, hq, :], wqf.at[o, hq, :]) for o in (1, 3)], wqf.at[0:2, 0:HALF, :])
    got_wqo()
    for o in (1, 3):
        q[o] = dot(frows[...], wqf[o]).astype(BF)
    got_kvo = {}

    def pass_on(o):
        got_k[o]()
        got_kvo[o] = to_other([(kvp.at[core, o], kvp.at[core, o])], kvp.at[0, o])

    lane = lax.broadcasted_iota(jnp.int32, (WIDTH, WIDTH), 1) // DH

    def only(h, a):
        return jnp.where(lane == h, a.astype(F32), 0.0).astype(BF)

    def forward(g):
        kg = kvp[0, g]
        vg_t = flip(kvp[1, g])
        qg = q[g]
        for h in range(4):
            scores = dot_nt(only(h, kg), qg)
            top = jnp.max(scores, axis=0, keepdims=True)
            e = jnp.exp((scores - top) * SCALE)
            p = (e * (1.0 / jnp.sum(e, axis=0, keepdims=True))).astype(BF)
            prob[4 * g + h] = p
            att_t[g, h * DH : (h + 1) * DH, :] = dot(vg_t[h * DH : (h + 1) * DH, :], p).astype(BF)
        att[g] = flip(att_t[g])

    pass_on(0)
    got_kvo[0]()
    forward(0)
    pass_on(1)
    got_wq2()
    got_wqo2 = to_other([(wqf.at[2, hq, :], wqf.at[2, hq, :])], wqf.at[0, 0:HALF, :])
    got_wof()
    got_woo = to_other([(wof.at[1:N_X, :, mine], wof.at[1:N_X, :, mine])], wof.at[1:N_X, :, 0:HALF])
    pass_on(3)
    got_kvo[1]()
    forward(1)
    pass_on(2)
    got_ff = gather(fx, ff.at[core, :, piece(chip), :], ff.at[0, :, 0:240, :])
    got_kvo[3]()
    forward(3)
    got_wqo2()
    q[2] = dot(frows[...], wqf[2]).astype(BF)
    got_kvo[2]()
    forward(2)

    def mix():
        @pl.loop(0, N_X)
        def _(n):
            at = block(beyond(n), WIDTH)
            heads = jnp.concatenate([att[o] for o in range(N_X)], axis=1)
            weights = jnp.concatenate([wof[o, :, at] for o in range(N_X)], axis=0)
            mix_s[n] = dot(heads, weights).astype(BF)

        arrived = to_x(lambda dx: mix_s.at[dx], lambda o: mix_r.at[my_rows, :], mix_r.at[0 : 3 * rows, :])
        return arrived, load(mix_s.at[0], mix_r.at[my_rows, :])

    for copy in in_c:
        copy.wait()
    got_cot()

    got_wpair, got_wa = ({}, {}), ({}, {})

    def to_pair(k, o):
        got_wpair[k][o] = to_other([(w_s.at[k, o, :, theirs], w_pair.at[k, o])], w_pair.at[k, o])

    def stage_a(k, o):
        got_wpair[k][o]()
        w_sum[k, o] = (w_s[k, o, :, mine].astype(F32) + w_pair[k, o].astype(F32)).astype(BF)
        got_wa[k][o] = to_line(
            lambda p: w_sum.at[k, o, block(p, 64), :], lambda d: w_ra.at[k, o, d], w_ra.at[k, o, 1:N_X], at_a, step_a
        )

    for o in range(N_X):
        w_s[0, o] = dot(att_t[o], cot[...]).astype(BF)
        to_pair(0, o)

    got_woo()

    @pl.loop(0, N_X)
    def _(g):
        ga[g] = dot_nt(cot[...], wof[g]).astype(BF)

    for o in range(N_X):
        stage_a(0, o)

    got_wb, got_wx = ({}, {}), ({}, {})

    def stage_b(k, o):
        got_wa[k][o]()
        w_s2[k, o] = add(w_sum[k, o, block(at_a, 64), :], lambda d: w_ra[k, o, d], N_X)
        got_wb[k][o] = to_line(
            lambda p: w_s2.at[k, o, piece(p), :], lambda d: w_rb.at[k, o, d], w_rb.at[k, o, 1:N_X], at_b, step_b
        )

    def stage_x(k, o):
        got_wb[k][o]()
        w_x[k, o] = add(w_s2[k, o, piece(at_b), :], lambda d: w_rb[k, o, d], N_X)
        if o:
            got_wx[k][o] = to_x(lambda dx: w_x.at[k, dx], lambda d: w_xr.at[k, d], w_xr.at[k, N_X - o], (o,))

    def stage_w(k):
        for o in (1, 2, 3):
            got_wx[k][o]()
        w_f[k] = add(w_x[k, 0], lambda o: w_xr[k, o], N_X)
        return gather(w_f.at[k], w_ag.at[k, core, piece(4 * at_a + at_b), :], w_ag.at[k, 0, 0:240, :])

    got_ff()
    got_ffo = to_other([(ff.at[core], ff.at[core])], ff.at[0])

    def backward(g):
        vg = kvp[1, g]
        kg_t = flip(kvp[0, g])
        qg = q[g]
        gag = ga[g]
        gk = jnp.zeros((WIDTH, WIDTH), F32)
        gv = jnp.zeros((WIDTH, WIDTH), F32)
        for h in range(4):
            pb = prob[4 * g + h]
            p = pb.astype(F32)
            gp = dot_nt(only(h, vg), gag)
            inner = jnp.sum(p * gp, axis=0, keepdims=True)
            gs = (p * (gp - inner) * SCALE).astype(BF)
            gq_t[g, h * DH : (h + 1) * DH, :] = dot(kg_t[h * DH : (h + 1) * DH, :], gs).astype(BF)
            gk = jnp.where(lane == h, dot(gs, qg), gk)
            gv = jnp.where(lane == h, dot(pb, gag), gv)
        gkv[0, g] = gk.astype(BF)
        gkv[1, g] = gv.astype(BF)
        gq[g] = flip(gq_t[g])

    order = (1, 2, 3, 0)
    got_gpair, got_grs, got_gx = {}, {}, {}

    def pair_sums(o):
        got_gpair[o]()
        gkv_sum[o] = (gkv[core, o].astype(F32) + gkv_pair[o].astype(F32)).astype(BF)
        got_grs[o] = to_chips(
            lambda j: gkv_sum.at[o, piece(j), :], lambda d: gkv_rs.at[o, d], gkv_rs.at[o, 1:N_CHIP]
        )
        stage_a(1, o)

    def chip_sums(o):
        got_grs[o]()
        gkv_x[o] = add(gkv_sum[o, piece(chip), :], lambda d: gkv_rs[o, d], N_CHIP)
        if o:
            got_gx[o] = to_x(lambda dx: gkv_x.at[dx], lambda d: gkv_xr.at[d], gkv_xr.at[N_X - o], (o,))

    for i, o in enumerate(order):
        backward(o)
        got_gpair[o] = to_other([(gkv.at[1 - core, o], gkv_pair.at[o])], gkv_pair.at[o])
        w_s[1, o] = dot(gq_t[o], frows[...]).astype(BF)
        to_pair(1, o)
        if i == 0:
            got_mix, own_mix = mix()
        if i > 0:
            pair_sums(order[i - 1])
        if i > 1:
            chip_sums(order[i - 2])
        if i == 2:
            for g in range(N_X):
                stage_b(0, g)
        if i > 1:
            stage_b(1, order[i - 2])
    pair_sums(order[3])
    chip_sums(order[2])
    for g in range(N_X):
        stage_x(0, g)
    stage_b(1, order[2])
    for o in order[:2]:
        stage_x(1, o)

    @pl.loop(0, N_X)
    def _(n):
        at = block(beyond(n), WIDTH)
        heads = jnp.concatenate([gq[o] for o in range(N_X)], axis=1)
        weights = jnp.concatenate([wqf[o, at, :] for o in range(N_X)], axis=1)
        gf_s[n] = dot_nt(heads, weights).astype(BF)

    def send_gf(which):
        return to_x(
            lambda dx: gf_s.at[dx], lambda o: gf_r.at[my_rows, :], gf_r.at[0 : len(which) * rows, :], which
        )

    got_gf = [send_gf((1, 3))]
    own_gf = load(gf_s.at[0], gf_r.at[my_rows, :])

    chip_sums(0)
    for o in (1, 2, 3):
        got_gx[o]()
    gk16[0] = add(gkv_x[0], lambda o: gkv_xr[o], N_X)
    for o in range(N_X):
        m_s[o] = dot_nt(gk16[0], wkv[core, block(beyond(o), WIDTH), :]).astype(BF)
    got_m = to_x(lambda dx: m_s.at[dx], lambda o: m_r.at[o], m_r.at[1:N_X])
    got_w = [stage_w(0)]
    stage_b(1, 0)
    stage_x(1, order[2])
    got_m()
    gk16[1] = add(m_s[0], lambda o: m_r[o], N_X)
    got_gkm = gather(gk16, gkm.at[core, :, piece(chip), :], gkm.at[0, :, 0:240, :])
    got_gf.append(send_gf((2,)))
    outs = []
    stage_x(1, 0)
    got_w.append(stage_w(1))
    got_gkm()
    got_gkmo = to_other([(gkm.at[core], gkm.at[core])], gkm.at[0])
    got_w[0]()
    got_wo2 = [to_other([(w_ag.at[0, core], w_ag.at[0, core])], w_ag.at[0, 0])]
    own_mix.wait()
    got_mix()
    outs.append(load(mix_r, mixed_o))
    got_ffo()
    got_gkmo()

    @pl.loop(0, N_X)
    def _(o):
        at = block(beyond(o), WIDTH)
        gwk_v[at, :] = dot(flip(ff[0, o]), gkm[0, 0]).astype(BF)
        gwv_v[at, :] = dot(flip(ff[1, o]), gkm[1, 0]).astype(BF)

    outs.append(load(gwk_v, gwk_o))
    outs.append(load(gwv_v, gwv_o))
    own_gf.wait()
    for wait in got_gf:
        wait()

    @pl.loop(0, N_X)
    def _(b):
        at = block(b, rows)
        total = gf_r[at, :].astype(F32) + dot(len_t[0, at, :], gkm[0, 1]) + dot(len_t[1, at, :], gkm[1, 1])
        gf_r[at, :] = total.astype(BF)

    outs.append(load(gf_r, gframes_o))
    got_wo2[0]()
    outs.append(load(w_ag.at[0], gw_o.at[0]))
    got_w[1]()
    got_wo2.append(to_other([(w_ag.at[1, core], w_ag.at[1, core])], w_ag.at[1, 0]))
    got_wo2[1]()
    outs.append(load(w_ag.at[1], gw_o.at[1]))
    for ref, sem in sent:
        landed(ref, sem)
    for copy in outs:
        copy.wait()


def finish(
    mixed, gframes, gwk, gwv, gw,
    mixed_o, gframes_o, gwq_o, gwk_o, gwv_o, gwo_o,
    raw_k, raw_w, raw_f, wide, wide_o, sem_ref,
):
    sems = Sems(sem_ref)

    def copy(src, dst):
        c = pltpu.make_async_copy(src, dst, sems.new())
        c.start()
        return c

    ins = [copy(gwk, raw_k.at[0]), copy(gwv, raw_k.at[1]), copy(gw.at[0], raw_w.at[0]), copy(gw.at[1], raw_w.at[1])]
    through = [copy(mixed, raw_f.at[0]), copy(gframes, raw_f.at[1])]
    outs = []
    for k, out in enumerate((gwk_o, gwv_o)):
        ins[k].wait()
        wide[k] = raw_k[k].astype(F32)
        outs.append(copy(wide.at[k], out))
    for k, out in enumerate((mixed_o, gframes_o)):
        through[k].wait()
        outs.append(copy(raw_f.at[k], out))
    ins[2].wait()
    for t in range(2):
        wide_o[:, t * HALF : (t + 1) * HALF] = raw_w[0, t].astype(F32)
    outs.append(copy(wide_o, gwo_o))
    ins[3].wait()
    for t in range(2):
        wide[2, t * HALF : (t + 1) * HALF, :] = raw_w[1, t].astype(F32).T
    outs.append(copy(wide.at[2], gwq_o))
    for c in outs:
        c.wait()


def body(frames, len_keys, len_values, w_query, w_key, w_value, w_out, cotangent):
    span, depth = frames.shape
    rows = span // N_X

    def bf(*shape):
        return pltpu.VMEM(shape, BF)

    scratch = [
        bf(span, 256), bf(rows, depth), bf(2, 256, span), bf(2, span, 256),
        bf(4, 1024, 256), bf(4, 256, 1024), bf(4, 16, 512), bf(2, 1024, 256), bf(rows, depth),
        bf(2, 256, 256), bf(256, 256), bf(256, 256), bf(16, 16, 256),
        bf(4, 16, 256), bf(4, 16, 256), bf(2, 4, 256, 256), bf(2, 4, 256, 256),
        bf(4, rows, 256), bf(4, rows, 256), bf(16, 256, rows),
        bf(4, 256, rows), bf(4, rows, 256), bf(4, 256, rows), bf(4, rows, 256),
        bf(4, rows, 256), bf(span, 256), bf(4, rows, 256), bf(span, 256),
        bf(2, 4, 256, 256), bf(4, 256, 256), bf(4, 256, 256), bf(4, 16, 16, 256),
        bf(4, 16, 256), bf(4, 16, 256), bf(2, 16, 256), bf(4, 16, 256), bf(4, 16, 256),
        bf(2, 2, 256, 256),
        bf(2, 4, 256, 1024), bf(2, 4, 256, 512), bf(2, 4, 256, 512), bf(2, 4, 4, 64, 512),
        bf(2, 4, 64, 512), bf(2, 4, 4, 16, 512), bf(2, 4, 16, 512), bf(2, 4, 16, 512),
        bf(2, 16, 512), bf(2, 2, 256, 512), bf(depth, 256), bf(depth, 256),
        pltpu.SemaphoreType.DMA((220,)),
    ]
    any_ = pl.BlockSpec(memory_space=pl.ANY)
    shape = jax.ShapeDtypeStruct
    raw = pl.pallas_call(
        kernel,
        out_shape=(
            shape((span, 256), BF), shape((span, 256), BF),
            shape((depth, 256), BF), shape((depth, 256), BF), shape((2, 2, 256, 512), BF),
        ),
        in_specs=[any_] * 8,
        out_specs=(any_,) * 5,
        scratch_shapes=scratch,
        compiler_params=pltpu.CompilerParams(
            collective_id=0, has_side_effects=True, vmem_limit_bytes=60 * 1024 * 1024
        ),
        cost_estimate=pl.CostEstimate(flops=14_000_000_000, bytes_accessed=24_000_000, transcendentals=2_097_152),
    )(frames, len_keys, len_values, w_query, w_key, w_value, w_out, cotangent)
    return pl.pallas_call(
        finish,
        out_shape=(
            shape((span, 256), BF), shape((span, 256), BF),
            shape((depth, 256), F32), shape((depth, 256), F32), shape((depth, 256), F32), shape((256, depth), F32),
        ),
        in_specs=[any_] * 5,
        out_specs=(any_,) * 6,
        scratch_shapes=[
            bf(2, depth, 256), bf(2, 2, 256, 512), bf(2, span, 256),
            pltpu.VMEM((3, depth, 256), F32), pltpu.VMEM((256, depth), F32),
            pltpu.SemaphoreType.DMA((12,)),
        ],
        compiler_params=pltpu.CompilerParams(vmem_limit_bytes=60 * 1024 * 1024),
        cost_estimate=pl.CostEstimate(flops=1_000_000, bytes_accessed=11_000_000, transcendentals=0),
    )(*raw)


def solution(mesh):
    placed = (
        P("ctx", None),
        P(None, "ctx"),
        P(None, "ctx"),
        P(None, "head"),
        P(None, "head"),
        P(None, "head"),
        P("head", None),
        P("ctx", "head"),
    )
    return jax.shard_map(
        body,
        mesh=mesh,
        in_specs=placed,
        out_specs=(
            P("ctx", "head"),
            P("ctx", "head"),
            P(None, "head"),
            P(None, "head"),
            P(None, "head"),
            P("head", None),
        ),
        check_vma=False,
    )
```

```python
import jax
import jax.numpy as jnp
from jax import lax
from jax.experimental import pallas as pl
from jax.experimental.pallas import tpu as pltpu
from jax.sharding import PartitionSpec as P

DH = 64
SCALE = DH ** -0.5
N_X = 4
N_CHIP = 16
WIDTH = 256
HALF = 512
MESH = pl.DeviceIdType.MESH
BF = jnp.bfloat16
F32 = jnp.float32


def dot(a, b):
    return jnp.dot(a, b, preferred_element_type=F32)


def dot_nt(a, b):
    return lax.dot_general(a, b, (((1,), (1,)), ((), ())), preferred_element_type=F32)


def flip(a):
    return a.astype(F32).T.astype(BF)


class Sems:
    def __init__(self, ref):
        self.ref, self.used = ref, 0

    def new(self):
        self.used += 1
        return self.ref.at[self.used - 1]


def kernel(
    frames, len_keys, len_values, w_query, w_key, w_value, w_out, cotangent,
    mixed_o, gframes_o, gwk_o, gwv_o, gw_o,
    fcols, frows, lens, len_t, wqf, wof, wo_p, wkv, cot,
    fpart, fpair, fsum, frs, fx, kpx, ff, kvp,
    q, ga, prob, att_t, att, gq_t, gq,
    mix_s, mix_r, gf_s, gf_r,
    gkv, gkv_pair, gkv_sum, gkv_rs, gkv_x, gkv_xr, gk16, m_s, m_r, gkm,
    w_s, w_pair, w_sum, w_ra, w_s2, w_rb, w_x, w_xr, w_f, w_ag, gwk_v, gwv_v, sem_ref,
):
    sems = Sems(sem_ref)
    me = lax.axis_index("ctx")
    x = lax.axis_index("head")
    core = lax.rem(me, 2)
    chip = lax.div(me, 2)
    other = me + 1 - 2 * core
    rows = frows.shape[0]
    step_a = 1 + 3 * core
    step_b = 4 - 3 * core
    at_a = lax.rem(lax.div(chip, step_a), N_X)
    at_b = lax.rem(lax.div(chip, step_b), N_X)

    def block(i, size):
        return pl.ds(pl.multiple_of(i * size, size), size)

    def beyond(o):
        return lax.rem(x + o, N_X)

    def piece(i):
        return block(i, 16)

    my_cols = block(x, WIDTH)
    my_rows = block(x, rows)
    mine = block(core, HALF)
    theirs = block(1 - core, HALF)
    hq = block(core, HALF)

    def load(src, dst):
        copy = pltpu.make_async_copy(src, dst, sems.new())
        copy.start()
        return copy

    in_f = [load(frames.at[:, my_cols], fcols), load(len_keys, lens.at[0]), load(len_values, lens.at[1])]
    in_w = [load(w_out, wof.at[0])]
    in_k = [load(w_key, wkv.at[0]), load(w_value, wkv.at[1])]
    in_q = [load(frames.at[my_rows, :], frows), load(w_query, wqf.at[0])]
    in_c = [load(cotangent.at[my_rows, :], cot.at[:, my_cols])]

    barrier = pltpu.get_barrier_semaphore()
    pl.semaphore_signal(barrier, inc=1, device_id=(other, x), device_id_type=MESH)
    for dx in range(1, N_X):
        pl.semaphore_signal(barrier, inc=1, device_id=(me, beyond(dx)), device_id_type=MESH)

    @pl.loop(1, N_CHIP)
    def _(d):
        pl.semaphore_signal(
            barrier, inc=1, device_id=(lax.rem(me + 2 * d, 2 * N_CHIP), x), device_id_type=MESH
        )

    for copy in in_f:
        copy.wait()

    @pl.loop(0, 2)
    def _(t):
        fpart[t] = dot(lens[t], fcols[...]).astype(BF)

    pl.semaphore_wait(barrier, 1 + (N_X - 1) + (N_CHIP - 1))

    sent = []

    def landed(ref, sem):
        pltpu.make_async_copy(ref, ref, sem).wait()

    def remote(src, dst, s, r, device):
        pltpu.make_async_remote_copy(src, dst, s, r, device_id=device, device_id_type=MESH).start()

    def to_other(pairs, whole):
        s, r = sems.new(), sems.new()
        for src, dst in pairs:
            remote(src, dst, s, r, (other, x))
        sent.append((whole, s))
        return lambda: landed(whole, r)

    def to_x(src, dst, whole, which=(1, 3, 2)):
        s, r = sems.new(), sems.new()
        for dx in which:
            remote(src(dx), dst(N_X - dx), s, r, (me, beyond(dx)))
        sent.append((whole, s))
        return lambda: landed(whole, r)

    def to_chips(src, dst, whole):
        s, r = sems.new(), sems.new()

        @pl.loop(1, N_CHIP)
        def _(d):
            peer = lax.rem(chip + d, N_CHIP)
            remote(src(peer), dst(N_CHIP - d), s, r, (2 * peer + core, x))

        sent.append((whole, s))
        return lambda: landed(whole, r)

    def to_line(src, dst, whole, at, step):
        s, r = sems.new(), sems.new()
        for d in (1, 3, 2):
            peer = lax.rem(at + d, N_X)
            remote(src(peer), dst(N_X - d), s, r, (me + 2 * step * (peer - at), x))
        sent.append((whole, s))
        return lambda: landed(whole, r)

    def gather(src, full, fifteen):
        copy = load(src, full)
        done = to_chips(lambda j: src, lambda o: full, fifteen)

        def arrive():
            copy.wait()
            done()

        return arrive

    def add(first, slots, count):
        total = first.astype(F32)
        for o in range(1, count):
            total = total + slots(o).astype(F32)
        return total.astype(BF)

    got_f = to_other([(fpart.at[1 - core], fpair)], fpair)
    got_wo = to_x(lambda dx: w_out.at[piece(chip), mine], lambda o: wo_p.at[o], wo_p.at[1:N_X])
    got_wq = to_x(
        lambda dx: w_query.at[hq, :], lambda o: wqf.at[o, hq, :], wqf.at[0:2, 0:HALF, :], (1, 3)
    )

    @pl.loop(0, 2)
    def _(t):
        @pl.loop(0, 4)
        def _(b):
            at = block(b, 512)
            len_t[t, at, :] = flip(lens[t, :, at])

    got_f()
    fsum[...] = (fpart[core].astype(F32) + fpair[...].astype(F32)).astype(BF)
    got_frs = to_chips(lambda j: fsum.at[piece(j), :], lambda o: frs.at[o], frs.at[1:N_CHIP])
    got_wo()
    got_wof = gather(
        wo_p.at[1:N_X], wof.at[1:N_X, piece(chip), mine], wof.at[1:N_X, 0:240, 0:HALF]
    )
    for copy in in_w:
        copy.wait()
    for copy in in_k + in_q:
        copy.wait()
    got_frs()
    fx[0] = add(fsum[piece(chip), :], lambda o: frs[o], N_CHIP)
    got_fx = to_x(lambda dx: fx.at[0], lambda o: fx.at[o], fx.at[1:N_X])
    q[0] = dot(frows[...], wqf[0]).astype(BF)
    got_fx()
    total = dot(fx[0], wkv[core, my_cols, :])
    for o in range(1, N_X):
        total = total + dot(fx[o], wkv[core, block(beyond(o), WIDTH), :])
    kpx[0] = total.astype(BF)
    got_kpx = to_x(lambda dx: kpx.at[0], lambda o: kpx.at[o], kpx.at[1:N_X])
    got_k = {0: gather(kpx.at[0], kvp.at[core, 0, piece(chip), :], kvp.at[0, 0, 0:240, :])}
    got_wq2 = to_x(lambda dx: w_query.at[hq, :], lambda o: wqf.at[o, hq, :], wqf.at[0, 0:HALF, :], (2,))
    got_cot = to_x(
        lambda dx: cotangent.at[block(beyond(dx), rows), :],
        lambda o: cot.at[:, my_cols],
        cot.at[:, 0 : 3 * WIDTH],
    )
    got_kpx()
    for o in (1, 3, 2):
        got_k[o] = gather(kpx.at[o], kvp.at[core, o, piece(chip), :], kvp.at[0, o, 0:240, :])

    got_wq()
    got_wqo = to_other([(wqf.at[o, hq, :], wqf.at[o, hq, :]) for o in (1, 3)], wqf.at[0:2, 0:HALF, :])
    got_wqo()
    for o in (1, 3):
        q[o] = dot(frows[...], wqf[o]).astype(BF)
    got_kvo = {}

    def pass_on(o):
        got_k[o]()
        got_kvo[o] = to_other([(kvp.at[core, o], kvp.at[core, o])], kvp.at[0, o])

    lane = lax.broadcasted_iota(jnp.int32, (WIDTH, WIDTH), 1) // DH

    def only(h, a):
        return jnp.where(lane == h, a.astype(F32), 0.0).astype(BF)

    def forward(g):
        kg = kvp[0, g]
        vg_t = flip(kvp[1, g])
        qg = q[g]
        for h in range(4):
            scores = dot_nt(only(h, kg), qg)
            top = jnp.max(scores, axis=0, keepdims=True)
            e = jnp.exp((scores - top) * SCALE)
            p = (e * (1.0 / jnp.sum(e, axis=0, keepdims=True))).astype(BF)
            prob[4 * g + h] = p
            att_t[g, h * DH : (h + 1) * DH, :] = dot(vg_t[h * DH : (h + 1) * DH, :], p).astype(BF)
        att[g] = flip(att_t[g])

    pass_on(0)
    got_kvo[0]()
    forward(0)
    pass_on(1)
    got_wq2()
    got_wqo2 = to_other([(wqf.at[2, hq, :], wqf.at[2, hq, :])], wqf.at[0, 0:HALF, :])
    got_wof()
    got_woo = to_other([(wof.at[1:N_X, :, mine], wof.at[1:N_X, :, mine])], wof.at[1:N_X, :, 0:HALF])
    pass_on(3)
    got_kvo[1]()
    forward(1)
    pass_on(2)
    got_ff = gather(fx, ff.at[core, :, piece(chip), :], ff.at[0, :, 0:240, :])
    got_kvo[3]()
    forward(3)
    got_wqo2()
    q[2] = dot(frows[...], wqf[2]).astype(BF)
    got_kvo[2]()
    forward(2)

    def mix():
        @pl.loop(0, N_X)
        def _(n):
            at = block(beyond(n), WIDTH)
            heads = jnp.concatenate([att[o] for o in range(N_X)], axis=1)
            weights = jnp.concatenate([wof[o, :, at] for o in range(N_X)], axis=0)
            mix_s[n] = dot(heads, weights).astype(BF)

        arrived = to_x(lambda dx: mix_s.at[dx], lambda o: mix_r.at[my_rows, :], mix_r.at[0 : 3 * rows, :])
        return arrived, load(mix_s.at[0], mix_r.at[my_rows, :])

    for copy in in_c:
        copy.wait()
    got_cot()

    got_wpair, got_wa = ({}, {}), ({}, {})

    def to_pair(k, o):
        got_wpair[k][o] = to_other([(w_s.at[k, o, :, theirs], w_pair.at[k, o])], w_pair.at[k, o])

    def stage_a(k, o):
        got_wpair[k][o]()
        w_sum[k, o] = (w_s[k, o, :, mine].astype(F32) + w_pair[k, o].astype(F32)).astype(BF)
        got_wa[k][o] = to_line(
            lambda p: w_sum.at[k, o, block(p, 64), :], lambda d: w_ra.at[k, o, d], w_ra.at[k, o, 1:N_X], at_a, step_a
        )

    for o in range(N_X):
        w_s[0, o] = dot(att_t[o], cot[...]).astype(BF)
        to_pair(0, o)

    got_woo()

    @pl.loop(0, N_X)
    def _(g):
        ga[g] = dot_nt(cot[...], wof[g]).astype(BF)

    for o in range(N_X):
        stage_a(0, o)

    def stage_b(k):
        for o in range(N_X):
            got_wa[k][o]()

        @pl.loop(0, N_X)
        def _(g):
            w_s2[k, g] = add(w_sum[k, g, block(at_a, 64), :], lambda o: w_ra[k, g, o], N_X)

        return to_line(
            lambda p: w_s2.at[k, :, piece(p), :], lambda o: w_rb.at[k, o], w_rb.at[k, 1:N_X], at_b, step_b
        )

    def stage_x(k):
        got_wb[k]()
        w_x[k] = add(w_s2[k, :, piece(at_b), :], lambda o: w_rb[k, o], N_X)
        return to_x(lambda dx: w_x.at[k, dx], lambda o: w_xr.at[k, o], w_xr.at[k, 1:N_X])

    def stage_w(k):
        got_wx[k]()
        w_f[k] = add(w_x[k, 0], lambda o: w_xr[k, o], N_X)
        return gather(w_f.at[k], w_ag.at[k, core, piece(4 * at_a + at_b), :], w_ag.at[k, 0, 0:240, :])

    got_ff()
    got_ffo = to_other([(ff.at[core], ff.at[core])], ff.at[0])

    def backward(g):
        vg = kvp[1, g]
        kg_t = flip(kvp[0, g])
        qg = q[g]
        gag = ga[g]
        gk = jnp.zeros((WIDTH, WIDTH), F32)
        gv = jnp.zeros((WIDTH, WIDTH), F32)
        for h in range(4):
            pb = prob[4 * g + h]
            p = pb.astype(F32)
            gp = dot_nt(only(h, vg), gag)
            inner = jnp.sum(p * gp, axis=0, keepdims=True)
            gs = (p * (gp - inner) * SCALE).astype(BF)
            gq_t[g, h * DH : (h + 1) * DH, :] = dot(kg_t[h * DH : (h + 1) * DH, :], gs).astype(BF)
            gk = jnp.where(lane == h, dot(gs, qg), gk)
            gv = jnp.where(lane == h, dot(pb, gag), gv)
        gkv[0, g] = gk.astype(BF)
        gkv[1, g] = gv.astype(BF)
        gq[g] = flip(gq_t[g])

    order = (1, 2, 3, 0)
    got_gpair, got_grs, got_gx = {}, {}, {}

    def pair_sums(o):
        got_gpair[o]()
        gkv_sum[o] = (gkv[core, o].astype(F32) + gkv_pair[o].astype(F32)).astype(BF)
        got_grs[o] = to_chips(
            lambda j: gkv_sum.at[o, piece(j), :], lambda d: gkv_rs.at[o, d], gkv_rs.at[o, 1:N_CHIP]
        )
        stage_a(1, o)

    def chip_sums(o):
        got_grs[o]()
        gkv_x[o] = add(gkv_sum[o, piece(chip), :], lambda d: gkv_rs[o, d], N_CHIP)
        if o:
            got_gx[o] = to_x(lambda dx: gkv_x.at[dx], lambda d: gkv_xr.at[d], gkv_xr.at[N_X - o], (o,))

    for i, o in enumerate(order):
        backward(o)
        got_gpair[o] = to_other([(gkv.at[1 - core, o], gkv_pair.at[o])], gkv_pair.at[o])
        w_s[1, o] = dot(gq_t[o], frows[...]).astype(BF)
        to_pair(1, o)
        if i == 0:
            got_mix, own_mix = mix()
        if i > 0:
            pair_sums(order[i - 1])
        if i > 1:
            chip_sums(order[i - 2])
        if i == 2:
            got_wb = [stage_b(0)]
    pair_sums(order[3])
    chip_sums(order[2])
    got_wx = [stage_x(0)]

    @pl.loop(0, N_X)
    def _(n):
        at = block(beyond(n), WIDTH)
        heads = jnp.concatenate([gq[o] for o in range(N_X)], axis=1)
        weights = jnp.concatenate([wqf[o, at, :] for o in range(N_X)], axis=1)
        gf_s[n] = dot_nt(heads, weights).astype(BF)

    def send_gf(which):
        return to_x(
            lambda dx: gf_s.at[dx], lambda o: gf_r.at[my_rows, :], gf_r.at[0 : len(which) * rows, :], which
        )

    got_gf = [send_gf((1, 3))]
    own_gf = load(gf_s.at[0], gf_r.at[my_rows, :])

    early = len(sent) - 2

    chip_sums(0)
    for o in (1, 2, 3):
        got_gx[o]()
    gk16[0] = add(gkv_x[0], lambda o: gkv_xr[o], N_X)
    for o in range(N_X):
        m_s[o] = dot_nt(gk16[0], wkv[core, block(beyond(o), WIDTH), :]).astype(BF)
    got_m = to_x(lambda dx: m_s.at[dx], lambda o: m_r.at[o], m_r.at[1:N_X])
    got_wb.append(stage_b(1))
    got_m()
    gk16[1] = add(m_s[0], lambda o: m_r[o], N_X)
    got_gkm = gather(gk16, gkm.at[core, :, piece(chip), :], gkm.at[0, :, 0:240, :])
    got_w = [stage_w(0)]
    got_wx.append(stage_x(1))
    got_gf.append(send_gf((2,)))
    outs = []
    got_w.append(stage_w(1))
    for ref, sem in sent[:early]:
        landed(ref, sem)
    del sent[:early]
    got_gkm()
    got_gkmo = to_other([(gkm.at[core], gkm.at[core])], gkm.at[0])
    got_w[0]()
    got_wo2 = [to_other([(w_ag.at[0, core], w_ag.at[0, core])], w_ag.at[0, 0])]
    own_mix.wait()
    got_mix()
    outs.append(load(mix_r, mixed_o))
    got_ffo()
    got_gkmo()

    @pl.loop(0, N_X)
    def _(o):
        at = block(beyond(o), WIDTH)
        gwk_v[at, :] = dot(flip(ff[0, o]), gkm[0, 0]).astype(BF)
        gwv_v[at, :] = dot(flip(ff[1, o]), gkm[1, 0]).astype(BF)

    outs.append(load(gwk_v, gwk_o))
    outs.append(load(gwv_v, gwv_o))
    own_gf.wait()
    for wait in got_gf:
        wait()

    @pl.loop(0, N_X)
    def _(b):
        at = block(b, rows)
        total = gf_r[at, :].astype(F32) + dot(len_t[0, at, :], gkm[0, 1]) + dot(len_t[1, at, :], gkm[1, 1])
        gf_r[at, :] = total.astype(BF)

    outs.append(load(gf_r, gframes_o))
    got_wo2[0]()
    outs.append(load(w_ag.at[0], gw_o.at[0]))
    got_w[1]()
    got_wo2.append(to_other([(w_ag.at[1, core], w_ag.at[1, core])], w_ag.at[1, 0]))
    got_wo2[1]()
    outs.append(load(w_ag.at[1], gw_o.at[1]))
    for ref, sem in sent:
        landed(ref, sem)
    for copy in outs:
        copy.wait()


def finish(
    mixed, gframes, gwk, gwv, gw,
    mixed_o, gframes_o, gwq_o, gwk_o, gwv_o, gwo_o,
    raw_k, raw_w, raw_f, wide, wide_o, sem_ref,
):
    sems = Sems(sem_ref)

    def copy(src, dst):
        c = pltpu.make_async_copy(src, dst, sems.new())
        c.start()
        return c

    ins = [copy(gwk, raw_k.at[0]), copy(gwv, raw_k.at[1]), copy(gw.at[0], raw_w.at[0]), copy(gw.at[1], raw_w.at[1])]
    through = [copy(mixed, raw_f.at[0]), copy(gframes, raw_f.at[1])]
    outs = []
    for k, out in enumerate((gwk_o, gwv_o)):
        ins[k].wait()
        wide[k] = raw_k[k].astype(F32)
        outs.append(copy(wide.at[k], out))
    for k, out in enumerate((mixed_o, gframes_o)):
        through[k].wait()
        outs.append(copy(raw_f.at[k], out))
    ins[2].wait()
    for t in range(2):
        wide_o[:, t * HALF : (t + 1) * HALF] = raw_w[0, t].astype(F32)
    outs.append(copy(wide_o, gwo_o))
    ins[3].wait()
    for t in range(2):
        wide[2, t * HALF : (t + 1) * HALF, :] = raw_w[1, t].astype(F32).T
    outs.append(copy(wide.at[2], gwq_o))
    for c in outs:
        c.wait()


def body(frames, len_keys, len_values, w_query, w_key, w_value, w_out, cotangent):
    span, depth = frames.shape
    rows = span // N_X

    def bf(*shape):
        return pltpu.VMEM(shape, BF)

    scratch = [
        bf(span, 256), bf(rows, depth), bf(2, 256, span), bf(2, span, 256),
        bf(4, 1024, 256), bf(4, 256, 1024), bf(4, 16, 512), bf(2, 1024, 256), bf(rows, depth),
        bf(2, 256, 256), bf(256, 256), bf(256, 256), bf(16, 16, 256),
        bf(4, 16, 256), bf(4, 16, 256), bf(2, 4, 256, 256), bf(2, 4, 256, 256),
        bf(4, rows, 256), bf(4, rows, 256), bf(16, 256, rows),
        bf(4, 256, rows), bf(4, rows, 256), bf(4, 256, rows), bf(4, rows, 256),
        bf(4, rows, 256), bf(span, 256), bf(4, rows, 256), bf(span, 256),
        bf(2, 4, 256, 256), bf(4, 256, 256), bf(4, 256, 256), bf(4, 16, 16, 256),
        bf(4, 16, 256), bf(4, 16, 256), bf(2, 16, 256), bf(4, 16, 256), bf(4, 16, 256),
        bf(2, 2, 256, 256),
        bf(2, 4, 256, 1024), bf(2, 4, 256, 512), bf(2, 4, 256, 512), bf(2, 4, 4, 64, 512),
        bf(2, 4, 64, 512), bf(2, 4, 4, 16, 512), bf(2, 4, 16, 512), bf(2, 4, 16, 512),
        bf(2, 16, 512), bf(2, 2, 256, 512), bf(depth, 256), bf(depth, 256),
        pltpu.SemaphoreType.DMA((180,)),
    ]
    any_ = pl.BlockSpec(memory_space=pl.ANY)
    shape = jax.ShapeDtypeStruct
    raw = pl.pallas_call(
        kernel,
        out_shape=(
            shape((span, 256), BF), shape((span, 256), BF),
            shape((depth, 256), BF), shape((depth, 256), BF), shape((2, 2, 256, 512), BF),
        ),
        in_specs=[any_] * 8,
        out_specs=(any_,) * 5,
        scratch_shapes=scratch,
        compiler_params=pltpu.CompilerParams(
            collective_id=0, has_side_effects=True, vmem_limit_bytes=60 * 1024 * 1024
        ),
        cost_estimate=pl.CostEstimate(flops=14_000_000_000, bytes_accessed=24_000_000, transcendentals=2_097_152),
    )(frames, len_keys, len_values, w_query, w_key, w_value, w_out, cotangent)
    return pl.pallas_call(
        finish,
        out_shape=(
            shape((span, 256), BF), shape((span, 256), BF),
            shape((depth, 256), F32), shape((depth, 256), F32), shape((depth, 256), F32), shape((256, depth), F32),
        ),
        in_specs=[any_] * 5,
        out_specs=(any_,) * 6,
        scratch_shapes=[
            bf(2, depth, 256), bf(2, 2, 256, 512), bf(2, span, 256),
            pltpu.VMEM((3, depth, 256), F32), pltpu.VMEM((256, depth), F32),
            pltpu.SemaphoreType.DMA((12,)),
        ],
        compiler_params=pltpu.CompilerParams(vmem_limit_bytes=60 * 1024 * 1024),
        cost_estimate=pl.CostEstimate(flops=1_000_000, bytes_accessed=11_000_000, transcendentals=0),
    )(*raw)


def solution(mesh):
    placed = (
        P("ctx", None),
        P(None, "ctx"),
        P(None, "ctx"),
        P(None, "head"),
        P(None, "head"),
        P(None, "head"),
        P("head", None),
        P("ctx", "head"),
    )
    return jax.shard_map(
        body,
        mesh=mesh,
        in_specs=placed,
        out_specs=(
            P("ctx", "head"),
            P("ctx", "head"),
            P(None, "head"),
            P(None, "head"),
            P(None, "head"),
            P("head", None),
        ),
        check_vma=False,
    )
```
